32 devices in a mesh: chain: 2 (over x), blk: 16 (over z, y, core).
Axes of the slice: x: 2, y: 2, z: 4, core: 2. Of those that a mesh axis runs over, the one named last changes fastest.
Arguments:
- ratings: bfloat16 [3, 65536, 768], P(None, ('chain', 'blk')), parts along dimension 1, may hold values from -4 to 4
- tile_mask: int32 [3, 512, 6], P(None, ('chain', 'blk')), parts along dimension 1, may hold values 0 or 1
- user_factors: float32 [65536, 256], P(('chain', 'blk')), parts along dimension 0, may hold values from -1.5 to 1.5
- user_momentum: float32 [65536, 256], P(('chain', 'blk')), parts along dimension 0, may hold values from -6 to 6
- item_factors: float32 [24576, 256], P(('chain', 'blk')), parts along dimension 0, may hold values from -1.5 to 1.5
- item_momentum: float32 [24576, 256], P(('chain', 'blk')), parts along dimension 0, may hold values from -6 to 6
- user_noise: bfloat16 [3, 65536, 256], P(None, ('chain', 'blk')), parts along dimension 1, may hold values from -6 to 6
- item_noise: bfloat16 [3, 24576, 256], P(None, ('chain', 'blk')), parts along dimension 1, may hold values from -6 to 6
- wishart_user: float32 [512, 256], P('chain'), parts along dimension 0, as said below
- wishart_item: float32 [512, 256], P('chain'), parts along dimension 0, as said below
Outputs:
- user_factors_out: float32 [65536, 256], P(('chain', 'blk')), parts along dimension 0
- user_momentum_out: float32 [65536, 256], P(('chain', 'blk')), parts along dimension 0
- item_factors_out: float32 [24576, 256], P(('chain', 'blk')), parts along dimension 0
- item_momentum_out: float32 [24576, 256], P(('chain', 'blk')), parts along dimension 0
- user_precision: float32 [512, 256], P('chain'), parts along dimension 0
- item_precision: float32 [512, 256], P('chain'), parts along dimension 0
The draws below stay inside these ranges and needn't reach their ends.
There are 2 independent parts, one for each index of `chain`. The reference program is written for one: setup_inputs(seed, part) draws one part's arguments, and reference() takes and returns one part's arrays. A program takes and returns all parts, laid end to end along the dimension named above; each array names one. Nothing has to cross between parts.
Inputs may be any that keep to these rules, and one draw needn't show every extreme that they name: `wishart_user`: lower triangular with a positive diagonal. `wishart_item`: lower triangular with a positive diagonal.
All inputs are finite; a program needn't handle non-finite values. No bound on the sum of `tile_mask` on one device may be relied on, other than what follows from the above.
Results may differ from the reference program's by a relative error of at most 0.00064.
Values sent between devices are 32-bit elements; how exact they have to be, the bound alone decides.
No kernel may reach another device: no remote copies, remote signals or barrier semaphores. Data moves between devices by JAX's collectives and lax.ppermute only.
A program may use at most 128 MiB of HBM per device.

```python
import jax
import jax.numpy as jnp
from jax import lax

K = 256
NU = 2048
NI = 768
TILE = 128
SUBSTEPS = 3
BLOCKS = 16
USERS = 32768
ITEMS = 12288


def triangle(key, offdiag, count):
    factor = jax.random.uniform(jax.random.fold_in(key, 5), (K,), minval=0.9, maxval=1.1)
    diagonal = jnp.sqrt((count + K - jnp.arange(K)).astype(jnp.float32)) * factor
    return jnp.tril(offdiag, -1) + jnp.diag(diagonal)


def draw_wishart_user(key, part):
    key = jax.random.fold_in(key, 11)
    second = jax.random.fold_in(key, 2)
    offdiag = jnp.clip(jax.random.normal(second, (K, K)), -5.0, 5.0)
    return triangle(key, offdiag, USERS)


def draw_wishart_item(key, part):
    key = jax.random.fold_in(key, 23)
    second = jax.random.fold_in(key, 2)
    offdiag = jnp.clip(jax.random.normal(second, (K, K)), -5.0, 5.0)
    return triangle(key, offdiag, ITEMS)


def plant(entries, own_key, low, largest):
    longest = entries.shape.index(max(entries.shape))
    spots = []
    for shift in (0, 1):
        where = [jax.random.randint(jax.random.fold_in(own_key, axis), (), 0, length) for axis, length in enumerate(entries.shape)]
        where[longest] = (where[longest] + shift) % entries.shape[longest]
        spots.append(tuple(where))
    return entries.at[spots[0]].set(low).at[spots[1]].set(largest)


def steps_of(stream_key, extent, split, smallest, high):
    def one(position, blocks):
        steps = jax.random.uniform(jax.random.fold_in(jax.random.fold_in(stream_key, 6), position), (blocks,), jnp.float32, smallest / len(split), high / len(split))
        return jnp.repeat(jnp.exp(steps), extent[position] // blocks).reshape((-1,) + (1,) * (len(extent) - position - 1))

    gain = one(*split[0])
    for cut in split[1:]:
        gain = gain * one(*cut)
    return gain


def centred(rng, dims, width, most, shards=(), held_as=jnp.bfloat16):
    factor_of = steps_of(rng, dims, shards, -0.22, 0.18) if shards else 1.0
    array = jax.random.normal(rng, dims, jnp.float32) * width * factor_of
    return jnp.minimum(jnp.maximum(array, -most), most).astype(held_as)


def setup_inputs(seed: int = 0, part: int = 0) -> dict:
    keys = jax.random.split(jax.random.key(seed), 11)
    part_keys = jax.random.split(jax.random.fold_in(keys[10], part), 11)
    return {
        "ratings": centred(part_keys[0], (SUBSTEPS, USERS, NI), 1.0, 4.0, ((1, 16),)),
        "tile_mask": plant((jax.random.randint(part_keys[1], (SUBSTEPS, USERS // TILE, NI // TILE), 0, 2) < 1).astype(jnp.int32), jax.random.fold_in(part_keys[1], 1), 0, 1),
        "user_factors": centred(part_keys[2], (USERS, K), 0.25, 1.5, ((0, 16),), jnp.float32),
        "user_momentum": centred(part_keys[3], (USERS, K), 1.0, 6.0, ((0, 16),), jnp.float32),
        "item_factors": centred(part_keys[4], (ITEMS, K), 0.25, 1.5, ((0, 16),), jnp.float32),
        "item_momentum": centred(part_keys[5], (ITEMS, K), 1.0, 6.0, ((0, 16),), jnp.float32),
        "user_noise": centred(part_keys[6], (SUBSTEPS, USERS, K), 1.0, 6.0, ((1, 16),)),
        "item_noise": centred(part_keys[7], (SUBSTEPS, ITEMS, K), 1.0, 6.0, ((1, 16),)),
        "wishart_user": draw_wishart_user(jax.random.fold_in(jax.random.fold_in(keys[10], part), 71), part),
        "wishart_item": draw_wishart_item(jax.random.fold_in(jax.random.fold_in(keys[10], part), 71), part),
    }


def refresh(gram, total, count, bartlett):
    mean = total / count
    outer = mean[:, None] * mean[None, :]
    scatter = jnp.eye(gram.shape[0], dtype=gram.dtype) + gram - count * count / (2.0 + count) * outer
    lower = jnp.linalg.cholesky(scatter)
    halfway = jax.scipy.linalg.solve_triangular(lower, bartlett, lower=True, trans=1)
    precision = jnp.dot(halfway.astype(jnp.float32), halfway.T.astype(jnp.float32), precision=lax.Precision.HIGHEST, preferred_element_type=jnp.float32)
    return (precision, count * mean / (2.0 + count))

def reference(ratings, tile_mask, user_factors, user_momentum, item_factors, item_momentum, user_noise, item_noise, wishart_user, wishart_item):
    highest = lax.Precision.HIGHEST
    gram_u = jnp.dot(user_factors.T.astype(jnp.float32), user_factors.astype(jnp.float32), precision=highest, preferred_element_type=jnp.float32)
    gram_i = jnp.dot(item_factors.T.astype(jnp.float32), item_factors.astype(jnp.float32), precision=highest, preferred_element_type=jnp.float32)
    precision_u, center_u = refresh(gram_u, lax.optimization_barrier(jnp.sum(user_factors, 0)), 1.0 * USERS, wishart_user)
    precision_i, center_i = refresh(gram_i, lax.optimization_barrier(jnp.sum(item_factors, 0)), 1.0 * ITEMS, wishart_item)
    users = user_factors.reshape(BLOCKS, NU, K)
    user_mom = user_momentum.reshape(BLOCKS, NU, K)
    items = item_factors.reshape(BLOCKS, NI, K)
    item_mom = item_momentum.reshape(BLOCKS, NI, K)
    weight = 1.0 * BLOCKS
    for substep in range(SUBSTEPS):
        rating_block = ratings[substep].reshape(BLOCKS, NU, NI).astype(jnp.float32)
        mask_block = tile_mask[substep].reshape(BLOCKS, NU // TILE, NI // TILE).astype(jnp.float32)
        low_u = users.astype(jnp.bfloat16).astype(jnp.float32)
        low_w = items.astype(jnp.bfloat16).astype(jnp.float32)
        predicted = jnp.einsum('bnk,bik->bni', low_u, low_w)
        masked = (rating_block - predicted).reshape(BLOCKS, NU // TILE, TILE, NI // TILE, TILE) * mask_block[:, :, None, :, None]
        residue = masked.reshape(BLOCKS, NU, NI).astype(jnp.bfloat16).astype(jnp.float32)
        like_u = jnp.einsum('bni,bik->bnk', residue, low_w)
        like_i = jnp.einsum('bni,bnk->bik', residue, low_u)
        prior_u = jnp.dot((users - center_u).reshape(-1, K).astype(jnp.float32), precision_u.astype(jnp.float32), precision=highest, preferred_element_type=jnp.float32).reshape(BLOCKS, NU, K)
        prior_i = jnp.dot((items - center_i).reshape(-1, K).astype(jnp.float32), precision_i.astype(jnp.float32), precision=highest, preferred_element_type=jnp.float32).reshape(BLOCKS, NI, K)
        noise_u = user_noise[substep].reshape(BLOCKS, NU, K).astype(jnp.float32)
        noise_i = item_noise[substep].reshape(BLOCKS, NI, K).astype(jnp.float32)
        user_mom = 0.8 * user_mom + 0.005 * (weight * like_u - prior_u) + jnp.sqrt(0.4) * noise_u
        users = users + 0.005 * user_mom
        item_mom = 0.8 * item_mom + 0.005 * (weight * like_i - prior_i) + jnp.sqrt(0.4) * noise_i
        items = items + 0.005 * item_mom
        items = jnp.roll(items, -1, axis=0)
        item_mom = jnp.roll(item_mom, -1, axis=0)
    return (users.reshape(USERS, K), user_mom.reshape(USERS, K), items.reshape(ITEMS, K), item_mom.reshape(ITEMS, K), precision_u, precision_i)
```

```python
import functools

import jax
import jax.numpy as jnp
from jax import lax
from jax.experimental import pallas as pl
from jax.experimental.pallas import tpu as pltpu
from jax.sharding import PartitionSpec as P

TILE = 128
SUBSTEPS = 3
RANK = 256
HALF = 128
LANES = 8
PACKED = 208
RATE = 0.005
DECAY = 0.8
HIGHEST = lax.Precision.HIGHEST
F32 = jnp.float32
BF16 = jnp.bfloat16
VMEM = pl.BlockSpec(memory_space=pltpu.VMEM)
SMEM = pl.BlockSpec(memory_space=pltpu.SMEM)


def dot(a, b, ca, cb, precision=None):
    return lax.dot_general(
        a, b, (((ca,), (cb,)), ((), ())), precision=precision, preferred_element_type=F32
    )


def params(mib=48):
    return pltpu.CompilerParams(vmem_limit_bytes=mib << 20)


def cost(flops, nbytes):
    return pl.CostEstimate(flops=int(flops), bytes_accessed=int(nbytes), transcendentals=0)


def gram_of(x):
    high = x.astype(BF16)
    rest = x - high.astype(F32)
    mid = rest.astype(BF16)
    low = (rest - mid.astype(F32)).astype(BF16)
    cross = dot(high, mid, 0, 0) + dot(high, low, 0, 0)
    return (dot(mid, mid, 0, 0) + (cross + cross.T)) + dot(high, high, 0, 0)


def store_packed(ref, gram, total):
    ref[0:HALF, 0:HALF] = gram[0:HALF, 0:HALF]
    ref[0:HALF, HALF:] = gram[HALF:, 0:HALF]
    ref[HALF : HALF + 64, 0:HALF] = gram[HALF : HALF + 64, HALF:]
    ref[HALF : HALF + 64, HALF:] = gram[HALF + 64 :, HALF:]
    ref[HALF + 64 :] = jnp.broadcast_to(total, (PACKED - HALF - 64, RANK))


def gram_kernel(core_ref, u_ref, w_ref, keep_ref, send_ref):
    first = core_ref[0] == 0
    user, item = u_ref[...], w_ref[...]
    gram_u, gram_i = gram_of(user), gram_of(item)
    total_u = jnp.sum(user, 0, keepdims=True)
    total_i = jnp.sum(item, 0, keepdims=True)
    store_packed(
        keep_ref, jnp.where(first, gram_u, gram_i), jnp.where(first, total_u, total_i)
    )
    store_packed(
        send_ref, jnp.where(first, gram_i, gram_u), jnp.where(first, total_i, total_u)
    )


def grams(core, users, items):
    out = jax.ShapeDtypeStruct((PACKED, RANK), F32)
    return pl.pallas_call(
        gram_kernel,
        out_shape=(out, out),
        in_specs=[SMEM, VMEM, VMEM],
        out_specs=(VMEM, VMEM),
        compiler_params=params(),
        cost_estimate=cost(
            8 * (users.shape[0] + items.shape[0]) * RANK * RANK,
            4 * (users.shape[0] + items.shape[0]) * RANK,
        ),
    )(core, users, items)


def inverse_factor(x):
    count = HALF // LANES
    shape = (LANES, HALF)
    rows = [x[LANES * q : LANES * (q + 1)] for q in range(count)]
    sub = lax.broadcasted_iota(jnp.int32, shape, 0)
    lane = lax.broadcasted_iota(jnp.int32, shape, 1)
    done = []
    for p in range(count):
        k = LANES * p
        cols = [
            [jnp.broadcast_to(rows[q][:, k + c : k + c + 1], shape) for q in range(p, count)]
            for c in range(LANES)
        ]
        panel = (lane >= k) & (lane < k + LANES)
        rows[p] = jnp.where(panel, jnp.where(lane - k == sub, 1.0, 0.0), rows[p])
        for q in range(p + 1, count):
            rows[q] = jnp.where(panel, 0.0, rows[q])
        scale = jnp.zeros(shape, F32)
        for i in range(LANES):
            pivot = jnp.broadcast_to(cols[i][0][i : i + 1], shape)
            inverse = 1.0 / pivot
            scale = jnp.where(sub == i, pivot, scale)
            factor = [v * inverse for v in cols[i]]
            factor[0] = jnp.where(sub > i, factor[0], 0.0)
            for c in range(i + 1, LANES):
                row = jnp.broadcast_to(cols[c][0][i : i + 1], shape)
                for q in range(count - p):
                    cols[c][q] = cols[c][q] - factor[q] * row
            row = jnp.broadcast_to(rows[p][i : i + 1], shape)
            for q in range(count - p):
                rows[p + q] = rows[p + q] - factor[q] * row
        done.append(jnp.where(lane < k + LANES, rows[p] * lax.rsqrt(scale), 0.0))
    return jnp.concatenate(done, 0)


def draw_kernel(core_ref, n_ref, mine_ref, other_ref, wu_ref, wi_ref, out_ref):
    first = core_ref[0] == 0
    lower = core_ref[1] == 0
    n = n_ref[0]
    mine, other = mine_ref[...], other_ref[...]
    packed = jnp.concatenate(
        [jnp.where(lower, mine, other), jnp.where(lower, other, mine)], 0
    )
    bartlett_top = jnp.where(first, wu_ref[0:HALF], wi_ref[0:HALF])
    bartlett_low = jnp.where(first, wu_ref[HALF:], wi_ref[HALF:])
    mean = packed[HALF + 64 : HALF + 72] / n
    outer = dot(mean * 0.125, mean, 0, 0, HIGHEST)
    factor = n * n / (2.0 + n)
    diag = lax.broadcasted_iota(jnp.int32, (HALF, HALF), 0) == lax.broadcasted_iota(
        jnp.int32, (HALF, HALF), 1
    )
    eye = jnp.where(diag, 1.0, 0.0)
    s11 = eye + packed[0:HALF, 0:HALF] - factor * outer[0:HALF, 0:HALF]
    s21 = packed[0:HALF, HALF:] - factor * outer[HALF:, 0:HALF]
    gram22 = jnp.concatenate(
        [packed[HALF : HALF + 64, 0:HALF], packed[HALF : HALF + 64, HALF:]], 0
    )
    s22 = eye + gram22 - factor * outer[HALF:, HALF:]
    g1 = inverse_factor(s11)
    l21 = dot(s21, g1, 1, 1, HIGHEST)
    s22 = s22 - dot(l21, l21, 1, 1, HIGHEST)
    top = dot(g1, bartlett_top, 0, 0, HIGHEST)
    carry = dot(l21, g1, 1, 0, HIGHEST)
    g2 = inverse_factor(s22)
    low = dot(g2, bartlett_low, 0, 0, HIGHEST)
    top = top - dot(carry, low, 0, 0, HIGHEST)
    both = jnp.concatenate([top, low], 0)
    out_ref[0:RANK] = dot(both, both, 1, 1, HIGHEST)
    out_ref[RANK:] = n * mean / (2.0 + n)


def draw(core, n, mine, other, wishart_user, wishart_item):
    return pl.pallas_call(
        draw_kernel,
        out_shape=jax.ShapeDtypeStruct((RANK + 8, RANK), F32),
        in_specs=[SMEM, SMEM, VMEM, VMEM, VMEM, VMEM],
        out_specs=VMEM,
        compiler_params=params(),
        cost_estimate=cost(10e9, 2e6),
    )(core, n, mine, other, wishart_user, wishart_item)


def residue_into(res_ref, ratings_ref, mask_ref, substep, tile, low_u, low_w):
    rows, items = res_ref.shape
    predicted = dot(low_u, low_w, 1, 1)
    for a in range(rows // TILE):
        for j in range(items // TILE):
            ra = slice(a * TILE, (a + 1) * TILE)
            ij = slice(j * TILE, (j + 1) * TILE)
            seen = mask_ref[substep, tile * (rows // TILE) + a, j].astype(F32)
            gap = ratings_ref[0, ra, ij].astype(F32) - predicted[ra, ij]
            res_ref[ra, ij] = (gap * seen).astype(BF16)


def first_kernel(
    weight,
    grid0,
    last,
    mask_ref,
    ratings_ref,
    u_ref,
    r_ref,
    un_ref,
    w_ref,
    q_ref,
    in_ref,
    acc_in_ref,
    _,
    rt_ref,
    acc_ref,
    res_ref,
    low_w_ref,
):
    step = pl.program_id(0)

    @pl.when(step == 0)
    def _():
        low_w_ref[...] = w_ref[...].astype(BF16)

    low_u = u_ref[...].astype(BF16)
    low_w = low_w_ref[...]
    residue_into(res_ref, ratings_ref, mask_ref, 0, grid0 + step, low_u, low_w)
    res = res_ref[...]
    like_u = dot(res, low_w, 1, 0)
    rt_ref[...] = (
        DECAY * r_ref[...] + RATE * weight * like_u + jnp.sqrt(0.4) * un_ref[0].astype(F32)
    )
    like_i = dot(low_u, res, 0, 0)

    @pl.when(step == 0)
    def _():
        acc_ref[...] = acc_in_ref[...] + like_i

    @pl.when(step > 0)
    def _():
        acc_ref[...] += like_i


def first_part(
    weight, part, parts, rows, mask, ratings, users, user_mom, user_noise, items, item_mom, acc, rt
):
    n, k = users.shape
    ni = items.shape[0]
    steps = n // rows // parts
    base = part * steps
    spec = pl.BlockSpec((rows, k), lambda i: (base + i, 0))
    deep = lambda w: pl.BlockSpec((1, rows, w), lambda i: (0, base + i, 0))
    whole = pl.BlockSpec((ni, k), lambda i: (0, 0))
    flat = pl.BlockSpec((k, ni), lambda i: (0, 0))
    kernel = functools.partial(first_kernel, weight, base, part == parts - 1)
    return pl.pallas_call(
        kernel,
        grid=(steps,),
        out_shape=(jax.ShapeDtypeStruct((n, k), F32), jax.ShapeDtypeStruct((k, ni), F32)),
        in_specs=[
            SMEM,
            deep(ni),
            spec,
            spec,
            deep(k),
            whole,
            pl.BlockSpec(memory_space=pl.ANY),
            pl.BlockSpec(memory_space=pl.ANY),
            flat,
            pl.BlockSpec(memory_space=pl.ANY),
        ],
        out_specs=(spec, flat),
        scratch_shapes=[pltpu.VMEM((rows, ni), BF16), pltpu.VMEM((ni, k), BF16)],
        input_output_aliases={9: 0},
        compiler_params=params(),
        cost_estimate=cost(6 * n // parts * ni * k, n // parts * (2 * ni + 14 * k)),
    )(mask, ratings, users, user_mom, user_noise, items, item_mom, item_mom, acc, rt)


def item_start_kernel(weight, q_ref, in_ref, acc_ref, out_ref):
    out_ref[...] = (
        DECAY * q_ref[...]
        + RATE * weight * acc_ref[...].T
        + jnp.sqrt(0.4) * in_ref[0].astype(F32)
    )


def item_start(weight, item_mom, item_noise, acc):
    ni, k = item_mom.shape
    return pl.pallas_call(
        functools.partial(item_start_kernel, weight),
        grid=(1,),
        out_shape=jax.ShapeDtypeStruct((ni, k), F32),
        in_specs=[
            pl.BlockSpec((ni, k), lambda i: (0, 0)),
            pl.BlockSpec((1, ni, k), lambda i: (0, 0, 0)),
            pl.BlockSpec((k, ni), lambda i: (0, 0)),
        ],
        out_specs=pl.BlockSpec((ni, k), lambda i: (0, 0)),
        compiler_params=params(),
        cost_estimate=cost(5 * ni * k, 14 * ni * k),
    )(item_mom, item_noise, acc)


def finish_kernel(users_, core_ref, mine_ref, other_ref, x_ref, mt_ref, x_out, m_out):
    take = (core_ref[0] == 0) == users_
    precision = jnp.where(take, mine_ref[0:RANK], other_ref[0:RANK])
    center = jnp.where(take, mine_ref[RANK : RANK + 1], other_ref[RANK : RANK + 1])
    x = x_ref[...]
    m = mt_ref[...] - RATE * dot(x - center, precision, 1, 0, HIGHEST)
    m_out[...] = m
    x_out[...] = x + RATE * m


def finish(is_user, rows, core, mine, other, x, partial):
    n, k = x.shape
    spec = pl.BlockSpec((rows, k), lambda i: (i, 0))
    whole = pl.BlockSpec((RANK + 8, k), lambda i: (0, 0))
    out = jax.ShapeDtypeStruct((n, k), F32)
    return pl.pallas_call(
        functools.partial(finish_kernel, is_user),
        grid=(n // rows,),
        out_shape=(out, out),
        in_specs=[SMEM, whole, whole, spec, spec],
        out_specs=(spec, spec),
        compiler_params=params(),
        cost_estimate=cost(12 * n * k * k, 16 * n * k),
    )(core, mine, other, x, partial)


def items_kernel(
    weight,
    substep,
    mask_ref,
    core_ref,
    mine_ref,
    other_ref,
    ratings_ref,
    u_ref,
    w_ref,
    q_ref,
    in_ref,
    res_ref,
    q_out,
    acc_ref,
    low_w_ref,
):
    step = pl.program_id(0)

    @pl.when(step == 0)
    def _():
        low_w_ref[...] = w_ref[...].astype(BF16)

    low_u = u_ref[...].astype(BF16)
    residue_into(res_ref, ratings_ref, mask_ref, substep, step, low_u, low_w_ref[...])
    like = dot(low_u, res_ref[...], 0, 0)

    @pl.when(step == 0)
    def _():
        acc_ref[...] = like

    @pl.when(step > 0)
    def _():
        acc_ref[...] += like

    @pl.when(step == pl.num_programs(0) - 1)
    def _():
        take = core_ref[0] != 0
        precision = jnp.where(take, mine_ref[0:RANK], other_ref[0:RANK])
        center = jnp.where(take, mine_ref[RANK : RANK + 1], other_ref[RANK : RANK + 1])
        prior = dot(w_ref[...] - center, precision, 1, 0, HIGHEST)
        q_out[...] = (
            DECAY * q_ref[...]
            + RATE * (weight * acc_ref[...].T - prior)
            + jnp.sqrt(0.4) * in_ref[0].astype(F32)
        )


def items_step(weight, substep, rows, mask, core, mine, other, ratings, users, w, q, item_noise):
    n, k = users.shape
    ni = w.shape[0]
    whole = pl.BlockSpec((ni, k), lambda i: (0, 0))
    prec = pl.BlockSpec((RANK + 8, k), lambda i: (0, 0))
    return pl.pallas_call(
        functools.partial(items_kernel, weight, substep),
        grid=(n // rows,),
        out_shape=(jax.ShapeDtypeStruct((n, ni), BF16), jax.ShapeDtypeStruct((ni, k), F32)),
        in_specs=[
            SMEM,
            SMEM,
            prec,
            prec,
            pl.BlockSpec((1, rows, ni), lambda i: (substep, i, 0)),
            pl.BlockSpec((rows, k), lambda i: (i, 0)),
            whole,
            whole,
            pl.BlockSpec((1, ni, k), lambda i: (substep, 0, 0)),
        ],
        out_specs=(pl.BlockSpec((rows, ni), lambda i: (i, 0)), whole),
        scratch_shapes=[pltpu.VMEM((k, ni), F32), pltpu.VMEM((ni, k), BF16)],
        compiler_params=params(),
        cost_estimate=cost(4 * n * ni * k, 4 * n * ni + 4 * n * k + 14 * ni * k),
    )(mask, core, mine, other, ratings, users, w, q, item_noise)


def users_kernel(
    weight, core_ref, mine_ref, other_ref, res_ref, w_ref, u_ref, r_ref, un_ref, u_out, r_out
):
    take = core_ref[0] == 0
    precision = jnp.where(take, mine_ref[0:RANK], other_ref[0:RANK])
    center = jnp.where(take, mine_ref[RANK : RANK + 1], other_ref[RANK : RANK + 1])
    u = u_ref[...]
    like = dot(res_ref[...], w_ref[...].astype(BF16), 1, 0)
    prior = dot(u - center, precision, 1, 0, HIGHEST)
    r = (
        DECAY * r_ref[...]
        + RATE * (weight * like - prior)
        + jnp.sqrt(0.4) * un_ref[0].astype(F32)
    )
    r_out[...] = r
    u_out[...] = u + RATE * r


def users_step(weight, substep, rows, core, mine, other, res, w, users, user_mom, user_noise):
    n, k = users.shape
    ni = w.shape[0]
    spec = pl.BlockSpec((rows, k), lambda i: (i, 0))
    prec = pl.BlockSpec((RANK + 8, k), lambda i: (0, 0))
    out = jax.ShapeDtypeStruct((n, k), F32)
    return pl.pallas_call(
        functools.partial(users_kernel, weight),
        grid=(n // rows,),
        out_shape=(out, out),
        in_specs=[
            SMEM,
            prec,
            prec,
            pl.BlockSpec((rows, ni), lambda i: (i, 0)),
            pl.BlockSpec((ni, k), lambda i: (0, 0)),
            spec,
            spec,
            pl.BlockSpec((1, rows, k), lambda i: (substep, i, 0)),
        ],
        out_specs=(spec, spec),
        compiler_params=params(),
        cost_estimate=cost(2 * n * ni * k + 12 * n * k * k, 2 * n * ni + 18 * n * k),
    )(core, mine, other, res, w, users, user_mom, user_noise)


def swapped(array, by, size):
    return lax.ppermute(array, "blk", [(i, i ^ by) for i in range(size)])


def local(
    ratings,
    tile_mask,
    user_factors,
    user_momentum,
    item_factors,
    item_momentum,
    user_noise,
    item_noise,
    wishart_user,
    wishart_item,
):
    blocks = lax.axis_size("blk")
    blk = lax.axis_index("blk")
    user_rows = user_factors.shape[0]
    item_rows = item_factors.shape[0]
    weight = 1.0 * blocks
    back = [(i, (i - 1) % blocks) for i in range(blocks)]
    shift = lambda array: lax.ppermute(array, "blk", back)
    fence = lax.optimization_barrier

    odd = blk % 2
    half = (blk // 2) % 2
    core = jnp.stack([odd, half]).astype(jnp.int32)
    n = jnp.where(odd == 0, 1.0 * user_rows * blocks, 1.0 * item_rows * blocks)
    n = n.astype(F32).reshape(1)

    rows = 256
    parts = 4
    rt = jnp.zeros(user_factors.shape, F32)
    acc = jnp.zeros((RANK, item_rows), F32)

    def part(j, acc, rt):
        rt, acc = first_part(
            weight,
            j,
            parts,
            rows,
            tile_mask,
            ratings,
            user_factors,
            user_momentum,
            user_noise,
            item_factors,
            item_momentum,
            acc,
            rt,
        )
        return acc, rt

    early_w = shift(item_factors)

    keep, send = grams(core, user_factors, item_factors)
    whole = keep + swapped(send, 1, blocks)
    rows_half = PACKED // 2
    mine = lax.dynamic_slice_in_dim(whole, half * rows_half, rows_half)
    send = lax.dynamic_slice_in_dim(whole, (1 - half) * rows_half, rows_half)
    by, j = 2, 0
    while by < blocks:
        send, acc, rt = fence((send, acc, rt))
        got = swapped(send, by, blocks)
        if j < parts:
            acc, rt = part(j, acc, rt)
            got, acc, rt = fence((got, acc, rt))
        mine = mine + got
        send = mine
        by, j = by * 2, j + 1
    send, acc, rt = fence((send, acc, rt))
    other = swapped(send, 2, blocks)
    while j < parts:
        acc, rt = part(j, acc, rt)
        j += 1
    item_part = item_start(weight, item_momentum, item_noise, acc)
    other, item_part, rt = fence((other, item_part, rt))
    early_q = shift(item_part)

    drawn = draw(core, n, mine, other, wishart_user, wishart_item)
    peer = swapped(drawn, 1, blocks)

    items, item_mom = finish(False, item_rows, core, drawn, peer, early_w, early_q)
    users, user_mom = finish(True, 512, core, drawn, peer, user_factors, rt)
    is_user = odd == 0
    precision_u = jnp.where(is_user, drawn[0:RANK], peer[0:RANK])
    precision_i = jnp.where(is_user, peer[0:RANK], drawn[0:RANK])

    for substep in range(1, SUBSTEPS):
        ahead = shift(items)
        res, item_next = items_step(
            weight,
            substep,
            rows,
            tile_mask,
            core,
            drawn,
            peer,
            ratings,
            users,
            items,
            item_mom,
            item_noise,
        )
        came = shift(item_next)
        users, user_mom = users_step(
            weight, substep, 512, core, drawn, peer, res, items, users, user_mom, user_noise
        )
        items = ahead + RATE * came
        item_mom = came
    return (users, user_mom, items, item_mom, precision_u, precision_i)


def solution(mesh):
    placed = (
        P(None, ("chain", "blk"), None),
        P(None, ("chain", "blk"), None),
        P(("chain", "blk"), None),
        P(("chain", "blk"), None),
        P(("chain", "blk"), None),
        P(("chain", "blk"), None),
        P(None, ("chain", "blk"), None),
        P(None, ("chain", "blk"), None),
        P("chain", None),
        P("chain", None),
    )
    return jax.shard_map(
        local,
        mesh=mesh,
        in_specs=placed,
        out_specs=(
            P(("chain", "blk"), None),
            P(("chain", "blk"), None),
            P(("chain", "blk"), None),
            P(("chain", "blk"), None),
            P("chain", None),
            P("chain", None),
        ),
        check_vma=False,
    )
```

```python
import functools

import jax
import jax.numpy as jnp
from jax import lax
from jax.experimental import pallas as pl
from jax.experimental.pallas import tpu as pltpu
from jax.sharding import PartitionSpec as P

TILE = 128
SUBSTEPS = 3
RANK = 256
HALF = 128
LANES = 8
PACKED = 208
RATE = 0.005
DECAY = 0.8
HIGHEST = lax.Precision.HIGHEST
F32 = jnp.float32
BF16 = jnp.bfloat16
VMEM = pl.BlockSpec(memory_space=pltpu.VMEM)
ANY = pl.BlockSpec(memory_space=pl.ANY)
SMEM = pl.BlockSpec(memory_space=pltpu.SMEM)


def dot(a, b, ca, cb, precision=None):
    return lax.dot_general(
        a, b, (((ca,), (cb,)), ((), ())), precision=precision, preferred_element_type=F32
    )


def params(mib=16):
    return pltpu.CompilerParams(vmem_limit_bytes=mib << 20)


def shape(rows, columns, dtype=F32):
    return jax.ShapeDtypeStruct((rows, columns), dtype)


def call(kernel, outs, in_specs, scratch=(), near=True):
    cost = pl.CostEstimate(flops=1000, bytes_accessed=1000, transcendentals=0)
    space = (lambda o: pltpu.VMEM(o.shape, o.dtype)) if near else (lambda o: o)
    run = pl.pallas_call(
        kernel,
        out_shape=jax.tree.map(space, outs),
        in_specs=in_specs,
        out_specs=jax.tree.map(lambda _: VMEM, outs),
        scratch_shapes=list(scratch),
        compiler_params=params(),
        cost_estimate=cost,
    )

    def placed(*args):
        spaces = {id(ANY): pltpu.HBM, id(VMEM): pltpu.VMEM}
        return run(
            *(
                pltpu.with_memory_space_constraint(a, spaces[id(s)]) if id(s) in spaces else a
                for a, s in zip(args, in_specs)
            )
        )

    return placed


def split(x):
    high = x.astype(BF16)
    rest = x - high.astype(F32)
    mid = rest.astype(BF16)
    low = (rest - mid.astype(F32)).astype(BF16)
    return high, mid, low


def split_rows(precision):
    high, mid, low = split(-precision)
    return jnp.concatenate([high, high, high, mid, mid, low], 0)


def split_columns(x):
    high, mid, low = split(x)
    return [high, mid, low, high, mid, high]


def gram_of(x):
    high, mid, low = split(x)
    cross = dot(high, mid, 0, 0) + dot(high, low, 0, 0)
    return (dot(mid, mid, 0, 0) + (cross + cross.T)) + dot(high, high, 0, 0)


def store_packed(ref, gram, total):
    ref[0:HALF, 0:HALF] = gram[0:HALF, 0:HALF]
    ref[0:HALF, HALF:] = gram[HALF:, 0:HALF]
    ref[HALF : HALF + 64, 0:HALF] = gram[HALF : HALF + 64, HALF:]
    ref[HALF : HALF + 64, HALF:] = gram[HALF + 64 :, HALF:]
    ref[HALF + 64 :] = jnp.broadcast_to(total, (PACKED - HALF - 64, RANK))


def gram_kernel(core_ref, mask_ref, u_hbm, w_hbm, *refs):
    sems = refs[-1]
    count = (len(refs) - 5) // 2
    others, (keep_ref, send_ref, u_ref, w_ref) = refs[:count], refs[count : count + 4]
    nears = refs[count + 4 : -1]
    first = core_ref[0] == 0
    rows = u_ref.shape[0] // 2
    copies = [pltpu.make_async_copy(w_hbm, w_ref, sems.at[0])]
    for j in range(2):
        part = pl.ds(j * rows, rows)
        copies.append(pltpu.make_async_copy(u_hbm.at[part], u_ref.at[part], sems.at[j + 1]))
    for j, (far, near) in enumerate(zip(others, nears)):
        source = far if len(far.shape) == 2 else far.at[0]
        copies.append(pltpu.make_async_copy(source, near, sems.at[j + 3]))
    for copy in copies:
        copy.start()
    copies[0].wait()
    item = w_ref[...]
    gram_i = gram_of(item)
    total_i = jnp.sum(item, 0, keepdims=True)
    gram_u, total_u = 0.0, 0.0
    for j in range(2):
        copies[j + 1].wait()
        user = u_ref[j * rows : (j + 1) * rows]
        gram_u += gram_of(user)
        total_u += jnp.sum(user, 0, keepdims=True)
    store_packed(
        keep_ref, jnp.where(first, gram_u, gram_i), jnp.where(first, total_u, total_i)
    )
    store_packed(
        send_ref, jnp.where(first, gram_i, gram_u), jnp.where(first, total_i, total_u)
    )
    for copy in copies[3:]:
        copy.wait()


def grams(core, mask, users, items, others):
    packed = shape(PACKED, RANK)
    nears = [shape(*x.shape[-2:], x.dtype) for x in others]
    return call(
        gram_kernel,
        (packed, packed, shape(*users.shape), shape(*items.shape), *nears),
        [SMEM, SMEM, ANY, ANY] + [ANY] * len(others),
        [pltpu.SemaphoreType.DMA((3 + len(others),))],
    )(core, mask, users, items, *others)


def halves_kernel(core_ref, keep_ref, got_ref, mine_ref, send_ref):
    lower = core_ref[1] == 0
    rows = mine_ref.shape[0]
    both = keep_ref[...] + got_ref[...]
    mine_ref[...] = jnp.where(lower, both[:rows], both[rows:])
    send_ref[...] = jnp.where(lower, both[rows:], both[:rows])


def halves(core, keep, got):
    half = shape(PACKED // 2, RANK)
    return call(halves_kernel, (half, half), [SMEM, VMEM, VMEM])(core, keep, got)


def sum_kernel(a_ref, b_ref, out_ref):
    out_ref[...] = a_ref[...] + b_ref[...]


def added(a, b):
    return call(sum_kernel, shape(*a.shape), [VMEM, VMEM])(a, b)


def inverse_factor(x):
    count = HALF // LANES
    tile = (LANES, HALF)
    rows = [x[LANES * q : LANES * (q + 1)] for q in range(count)]
    sub = lax.broadcasted_iota(jnp.int32, tile, 0)
    lane = lax.broadcasted_iota(jnp.int32, tile, 1)
    done = []
    for p in range(count):
        k = LANES * p
        cols = [
            [jnp.broadcast_to(rows[q][:, k + c : k + c + 1], tile) for q in range(p, count)]
            for c in range(LANES)
        ]
        panel = (lane >= k) & (lane < k + LANES)
        rows[p] = jnp.where(panel, jnp.where(lane - k == sub, 1.0, 0.0), rows[p])
        for q in range(p + 1, count):
            rows[q] = jnp.where(panel, 0.0, rows[q])
        scale = jnp.zeros(tile, F32)
        for i in range(LANES):
            pivot = jnp.broadcast_to(cols[i][0][i : i + 1], tile)
            inverse = 1.0 / pivot
            scale = jnp.where(sub == i, pivot, scale)
            factor = [v * inverse for v in cols[i]]
            factor[0] = jnp.where(sub > i, factor[0], 0.0)
            for c in range(i + 1, LANES):
                row = jnp.broadcast_to(cols[c][0][i : i + 1], tile)
                for q in range(count - p):
                    cols[c][q] = cols[c][q] - factor[q] * row
            row = jnp.broadcast_to(rows[p][i : i + 1], tile)
            for q in range(count - p):
                rows[p + q] = rows[p + q] - factor[q] * row
        done.append(jnp.where(lane < k + LANES, rows[p] * lax.rsqrt(scale), 0.0))
    return jnp.concatenate(done, 0)


def draw_kernel(counts, core_ref, mine_ref, other_ref, wu_ref, wi_ref, out_ref):
    first = core_ref[0] == 0
    lower = core_ref[1] == 0
    n = jnp.where(first, counts[0], counts[1])
    mine, other = mine_ref[...], other_ref[...]
    packed = jnp.concatenate(
        [jnp.where(lower, mine, other), jnp.where(lower, other, mine)], 0
    )
    bartlett_top = jnp.where(first, wu_ref[0:HALF], wi_ref[0:HALF])
    bartlett_low = jnp.where(first, wu_ref[HALF:], wi_ref[HALF:])
    mean = packed[HALF + 64 : HALF + 72] / n
    outer = dot(mean * 0.125, mean, 0, 0, HIGHEST)
    factor = n * n / (2.0 + n)
    diag = lax.broadcasted_iota(jnp.int32, (HALF, HALF), 0) == lax.broadcasted_iota(
        jnp.int32, (HALF, HALF), 1
    )
    eye = jnp.where(diag, 1.0, 0.0)
    s11 = eye + packed[0:HALF, 0:HALF] - factor * outer[0:HALF, 0:HALF]
    s21 = packed[0:HALF, HALF:] - factor * outer[HALF:, 0:HALF]
    gram22 = jnp.concatenate(
        [packed[HALF : HALF + 64, 0:HALF], packed[HALF : HALF + 64, HALF:]], 0
    )
    s22 = eye + gram22 - factor * outer[HALF:, HALF:]
    g1 = inverse_factor(s11)
    l21 = dot(s21, g1, 1, 1, HIGHEST)
    s22 = s22 - dot(l21, l21, 1, 1, HIGHEST)
    top = dot(g1, bartlett_top, 0, 0, HIGHEST)
    carry = dot(l21, g1, 1, 0, HIGHEST)
    g2 = inverse_factor(s22)
    low = dot(g2, bartlett_low, 0, 0, HIGHEST)
    top = top - dot(carry, low, 0, 0, HIGHEST)
    both = jnp.concatenate([top, low], 0)
    out_ref[0:RANK] = dot(both, both, 1, 1, HIGHEST)
    out_ref[RANK:] = n * mean / (2.0 + n)


def draw(counts, core, mine, other, wishart_user, wishart_item):
    return call(
        functools.partial(draw_kernel, counts),
        shape(RANK + 8, RANK),
        [SMEM, VMEM, VMEM, VMEM, VMEM],
    )(core, mine, other, wishart_user, wishart_item)


def prior_of(users, core_ref, mine_ref, other_ref):
    take = (core_ref[0] == 0) == users
    precision = jnp.where(take, mine_ref[0:RANK], other_ref[0:RANK])
    center = jnp.where(take, mine_ref[RANK : RANK + 1], other_ref[RANK : RANK + 1])
    return split_rows(precision), center


def residue_into(res_ref, at, ratings_ref, mask_ref, substep, row, rows, low_u, low_w):
    predicted = dot(low_u, low_w, 1, 1)
    for a in range(rows // TILE):
        for j in range(low_w.shape[0] // TILE):
            ra = slice(at + a * TILE, at + (a + 1) * TILE)
            pa = slice(a * TILE, (a + 1) * TILE)
            ij = slice(j * TILE, (j + 1) * TILE)
            seen = mask_ref[substep, j, (row + at) // TILE + a].astype(F32)
            gap = ratings_ref[ra, ij].astype(F32) - predicted[pa, ij]
            res_ref[ra, ij] = (gap * seen).astype(BF16)


def first_kernel(weight, row, slots, mask_ref, ratings_ref, r_ref, un_ref, u_ref, w_ref, *refs):
    count = len(slots)
    fars, (rt_ref, acc_ref) = refs[:count], refs[count : count + 2]
    nears = refs[count + 2 : 2 * count + 2]
    res_ref, low_ref, sems = refs[2 * count + 2 :]
    copies = [
        pltpu.make_async_copy(far.at[slot], near, sems.at[j])
        for j, (slot, far, near) in enumerate(zip(slots, fars, nears))
    ]
    for copy in copies:
        copy.start()
    low_w = w_ref[...].astype(BF16)
    total = rt_ref.shape[0]
    here = slice(row, row + total)
    low_ref[...] = u_ref[here].astype(BF16)
    rows = 256
    for t in range(total // rows):
        low_u = low_ref[t * rows : (t + 1) * rows]
        residue_into(
            res_ref, t * rows, ratings_ref.at[here], mask_ref, 0, row, rows, low_u, low_w
        )
    acc_ref[...] = dot(low_ref[...], res_ref[...], 0, 0)
    like_u = dot(res_ref[...], low_w, 1, 0)
    rt_ref[...] = (
        DECAY * r_ref[here]
        + RATE * weight * like_u
        + jnp.sqrt(0.4) * un_ref[here].astype(F32)
    )
    for copy in copies:
        copy.wait()


def first_part(weight, row, rows, mask, ratings, user_mom, user_noise, users, items, later):
    k = users.shape[1]
    ni = items.shape[0]
    slots = tuple(slot for slot, _ in later)
    fars = [far for _, far in later]
    rt, acc, *nears = call(
        functools.partial(first_kernel, weight, row, slots),
        (shape(rows, k), shape(k, ni), *(shape(*x.shape[1:], x.dtype) for x in fars)),
        [SMEM, VMEM, VMEM, VMEM, VMEM, VMEM] + [ANY] * len(fars),
        [
            pltpu.VMEM((rows, ni), BF16),
            pltpu.VMEM((rows, k), BF16),
            pltpu.SemaphoreType.DMA((max(len(fars), 1),)),
        ],
    )(mask, ratings, user_mom, user_noise, users, items, *fars)
    return rt, acc, nears


def item_start_kernel(weight, q_ref, in_ref, *refs):
    accs, out_ref = refs[:-1], refs[-1]
    like = accs[0][...]
    for acc in accs[1:]:
        like = like + acc[...]
    out_ref[...] = (
        DECAY * q_ref[...] + RATE * weight * like.T + jnp.sqrt(0.4) * in_ref[...].astype(F32)
    )


def item_start(weight, item_mom, item_noise, accs):
    return call(
        functools.partial(item_start_kernel, weight),
        shape(*item_mom.shape),
        [VMEM] * (2 + len(accs)),
    )(item_mom, item_noise, *accs)


def finish_kernel(is_user, pieces, core_ref, mine_ref, other_ref, *refs):
    (x_out, m_out, rhs_ref), ins = refs[-3:], refs[:-3]
    rhs, center = prior_of(is_user, core_ref, mine_ref, other_ref)
    rhs_ref[...] = rhs
    rows = 256
    read = lambda piece, at, size: ins[piece[0]][piece[1] + at : piece[1] + at + size]
    base = 0
    for size, factors, momenta in pieces:
        for at in range(0, size, rows):
            step = min(rows, size - at)
            x = read(factors, at, step)
            columns = jnp.concatenate(split_columns(x - center), 1)
            m = read(momenta, at, step) + RATE * dot(columns, rhs_ref[...], 1, 0)
            m_out[base : base + step] = m
            x_out[base : base + step] = x + RATE * m
            base += step


def finish(is_user, core, mine, other, arrays, pieces):
    n, k = sum(p[0] for p in pieces), arrays[0].shape[1]
    return call(
        functools.partial(finish_kernel, is_user, pieces),
        (shape(n, k), shape(n, k)),
        [SMEM] + [VMEM] * (2 + len(arrays)),
        [pltpu.VMEM((6 * RANK, k), BF16)],
    )(core, mine, other, *arrays)


def items_kernel(
    weight,
    substep,
    mask_ref,
    core_ref,
    mine_ref,
    other_ref,
    ratings_ref,
    u_ref,
    w_ref,
    q_ref,
    in_ref,
    res_ref,
    q_out,
    low_ref,
):
    low_w = w_ref[...].astype(BF16)
    rows = 256
    for t in range(u_ref.shape[0] // rows):
        here = slice(t * rows, (t + 1) * rows)
        low_u = u_ref[here].astype(BF16)
        low_ref[here] = low_u
        residue_into(res_ref, t * rows, ratings_ref, mask_ref, substep, 0, rows, low_u, low_w)
    like = dot(low_ref[...], res_ref[...], 0, 0)
    rhs, center = prior_of(False, core_ref, mine_ref, other_ref)
    prior = dot(jnp.concatenate(split_columns(w_ref[...] - center), 1), rhs, 1, 0)
    q_out[...] = (
        DECAY * q_ref[...]
        + RATE * (weight * like.T + prior)
        + jnp.sqrt(0.4) * in_ref[...].astype(F32)
    )


def items_step(weight, substep, mask, core, mine, other, ratings, users, w, q, item_noise):
    n, k = users.shape
    ni = w.shape[0]
    return call(
        functools.partial(items_kernel, weight, substep),
        (shape(n, ni, BF16), shape(ni, k)),
        [SMEM, SMEM] + [VMEM] * 7,
        [pltpu.VMEM((n, k), BF16)],
    )(mask, core, mine, other, ratings, users, w, q, item_noise)


def users_kernel(
    weight,
    core_ref,
    mine_ref,
    other_ref,
    res_ref,
    w_ref,
    u_ref,
    r_ref,
    un_ref,
    u_out,
    r_out,
    *refs,
):
    draws, rhs_ref = refs[:-1], refs[-1]
    if draws:
        mine, other = mine_ref[0:RANK], other_ref[0:RANK]
        first = core_ref[0] == 0
        draws[0][...] = jnp.where(first, mine, other)
        draws[1][...] = jnp.where(first, other, mine)
    ni = w_ref.shape[0]
    rhs_ref[0:ni] = w_ref[...].astype(BF16)
    rhs, center = prior_of(True, core_ref, mine_ref, other_ref)
    rhs_ref[ni:] = rhs
    rows = 256
    for t in range(u_ref.shape[0] // rows):
        here = slice(t * rows, (t + 1) * rows)
        x = u_ref[here]
        columns = jnp.concatenate(split_columns(x - center), 1)
        like = dot(res_ref[here], rhs_ref[0:ni], 1, 0)
        r = (
            DECAY * r_ref[here]
            + RATE * (weight * like + dot(columns, rhs_ref[ni:], 1, 0))
            + jnp.sqrt(0.4) * un_ref[here].astype(F32)
        )
        r_out[here] = r
        u_out[here] = x + RATE * r


def users_step(weight, last, core, mine, other, res, w, users, user_mom, user_noise):
    n, k = users.shape
    ni = w.shape[0]
    return call(
        functools.partial(users_kernel, weight),
        (shape(n, k), shape(n, k)) + (shape(RANK, RANK),) * (2 * last),
        [SMEM] + [VMEM] * 7,
        [pltpu.VMEM((ni + 6 * RANK, k), BF16)],
        near=not last,
    )(core, mine, other, res, w, users, user_mom, user_noise)


def arrived_kernel(w_ref, q_ref, w_out, q_out, sum_ref, sems):
    first = pltpu.make_async_copy(q_ref, q_out, sems.at[0])
    first.start()
    sum_ref[...] = w_ref[...] + RATE * q_ref[...]
    second = pltpu.make_async_copy(sum_ref, w_out, sems.at[1])
    second.start()
    first.wait()
    second.wait()


def arrived(before, came):
    out = pltpu.HBM(came.shape, F32)
    return pl.pallas_call(
        arrived_kernel,
        out_shape=(out, out),
        in_specs=[VMEM, VMEM],
        out_specs=(ANY, ANY),
        scratch_shapes=[pltpu.VMEM(came.shape, F32), pltpu.SemaphoreType.DMA((2,))],
        compiler_params=params(),
        cost_estimate=pl.CostEstimate(flops=1000, bytes_accessed=1000, transcendentals=0),
    )(before, came)


def swapped(array, by, size):
    return lax.ppermute(array, "blk", [(i, i ^ by) for i in range(size)])


def local(
    ratings,
    tile_mask,
    user_factors,
    user_momentum,
    item_factors,
    item_momentum,
    user_noise,
    item_noise,
    wishart_user,
    wishart_item,
):
    blocks = lax.axis_size("blk")
    blk = lax.axis_index("blk")
    user_rows = user_factors.shape[0]
    item_rows = item_factors.shape[0]
    weight = 1.0 * blocks
    back = [(i, (i - 1) % blocks) for i in range(blocks)]
    shift = lambda array: lax.ppermute(array, "blk", back)
    fence = lax.optimization_barrier

    odd = blk % 2
    half = (blk // 2) % 2
    core = jnp.stack([odd, half]).astype(jnp.int32)

    mask = tile_mask.transpose(0, 2, 1)
    parts = 4
    rows = user_rows // parts
    rts, accs, loaded = [], [], []
    later = [
        [(1, ratings)],
        [(2, ratings)],
        [(1, user_noise), (2, user_noise)],
        [(1, item_noise), (2, item_noise)],
    ]

    head = item_rows // 2
    early_w = shift(item_factors)

    keep, send, near_u, near_w, near_ratings, near_r, near_un, near_q, near_in, wu, wi = grams(
        core,
        mask,
        user_factors,
        item_factors,
        (
            ratings,
            user_momentum,
            user_noise,
            item_momentum,
            item_noise,
            wishart_user,
            wishart_item,
        ),
    )
    got = swapped(send, 1, blocks)
    mine, send = halves(core, keep, got)

    def part():
        j = len(rts)
        rt, acc, nears = first_part(
            weight,
            j * rows,
            rows,
            mask,
            near_ratings,
            near_r,
            near_un,
            near_u,
            near_w,
            later[j],
        )
        rts.append(rt)
        accs.append(acc)
        loaded.extend(nears)

    by = 2
    while by < blocks:
        send, near_u = fence((send, near_u))
        got = swapped(send, by, blocks)
        if len(rts) < parts:
            part()
            got, rts[-1], accs[-1] = fence((got, rts[-1], accs[-1]))
        if by == 2:
            got, early_w = fence((got, early_w))
        mine = added(mine, got)
        send = mine
        by = by * 2
    send, near_u = fence((send, near_u))
    other = swapped(send, 2, blocks)
    while len(rts) < parts:
        part()
    item_part = item_start(weight, near_q, near_in, accs)
    other, item_part, *rts = fence((other, item_part, *rts))
    early_q = shift(item_part)
    near_ratings = [None, *loaded[0:2]]
    near_un = [None, *loaded[2:4]]
    near_in = [None, *loaded[4:6]]

    counts = (1.0 * user_rows * blocks, 1.0 * item_rows * blocks)
    drawn = draw(counts, core, mine, other, wu, wi)
    peer = swapped(drawn, 1, blocks)

    users, user_mom = finish(
        True,
        core,
        drawn,
        peer,
        (near_u, *rts),
        tuple((rows, (0, j * rows), (1 + j, 0)) for j in range(parts)),
    )
    items, item_mom = finish(
        False,
        core,
        drawn,
        peer,
        (early_w, early_q),
        ((item_rows, (0, 0), (1, 0)),),
    )
    for substep in range(1, SUBSTEPS):
        last = substep == SUBSTEPS - 1
        before = shift(items)
        res, item_next = items_step(
            weight,
            substep,
            mask,
            core,
            drawn,
            peer,
            near_ratings[substep],
            users,
            items,
            item_mom,
            near_in[substep],
        )
        came = shift(item_next)
        users, user_mom, *precisions = users_step(
            weight, last, core, drawn, peer, res, items, users, user_mom, near_un[substep]
        )
        if not last:
            came, before, users, user_mom = fence((came, before, users, user_mom))
            items = before + RATE * came
            item_mom = came
    items, item_mom = arrived(before, came)
    return (users, user_mom, items, item_mom, *precisions)


def solution(mesh):
    placed = (
        P(None, ("chain", "blk"), None),
        P(None, ("chain", "blk"), None),
        P(("chain", "blk"), None),
        P(("chain", "blk"), None),
        P(("chain", "blk"), None),
        P(("chain", "blk"), None),
        P(None, ("chain", "blk"), None),
        P(None, ("chain", "blk"), None),
        P("chain", None),
        P("chain", None),
    )
    return jax.shard_map(
        local,
        mesh=mesh,
        in_specs=placed,
        out_specs=(
            P(("chain", "blk"), None),
            P(("chain", "blk"), None),
            P(("chain", "blk"), None),
            P(("chain", "blk"), None),
            P("chain", None),
            P("chain", None),
        ),
        check_vma=False,
    )
```

```python
import functools

import jax
import jax.numpy as jnp
from jax import lax
from jax.experimental import pallas as pl
from jax.experimental.pallas import tpu as pltpu
from jax.sharding import PartitionSpec as P

TILE = 128
SUBSTEPS = 3
RANK = 256
HALF = 128
LANES = 8
PACKED = 208
RATE = 0.005
DECAY = 0.8
HIGHEST = lax.Precision.HIGHEST
F32 = jnp.float32
BF16 = jnp.bfloat16
VMEM = pl.BlockSpec(memory_space=pltpu.VMEM)
ANY = pl.BlockSpec(memory_space=pl.ANY)
SMEM = pl.BlockSpec(memory_space=pltpu.SMEM)


def dot(a, b, ca, cb, precision=None):
    return lax.dot_general(
        a, b, (((ca,), (cb,)), ((), ())), precision=precision, preferred_element_type=F32
    )


def params(mib=16):
    return pltpu.CompilerParams(vmem_limit_bytes=mib << 20)


def shape(rows, columns, dtype=F32):
    return jax.ShapeDtypeStruct((rows, columns), dtype)


def call(kernel, outs, in_specs, scratch=(), near=True):
    cost = pl.CostEstimate(flops=1000, bytes_accessed=1000, transcendentals=0)
    space = (lambda o: pltpu.VMEM(o.shape, o.dtype)) if near else (lambda o: o)
    run = pl.pallas_call(
        kernel,
        out_shape=jax.tree.map(space, outs),
        in_specs=in_specs,
        out_specs=jax.tree.map(lambda _: VMEM, outs),
        scratch_shapes=list(scratch),
        compiler_params=params(),
        cost_estimate=cost,
    )

    def placed(*args):
        spaces = {id(ANY): pltpu.HBM, id(VMEM): pltpu.VMEM}
        return run(
            *(
                pltpu.with_memory_space_constraint(a, spaces[id(s)]) if id(s) in spaces else a
                for a, s in zip(args, in_specs)
            )
        )

    return placed


CHUNKS = 4


def fetches(slots, fars, nears, sems):
    copies = []
    for slot, far, near in zip(slots, fars, nears):
        source = far if slot is None else far.at[slot]
        rows = near.shape[0] // CHUNKS
        for c in range(CHUNKS):
            part = pl.ds(c * rows, rows)
            copies.append(
                pltpu.make_async_copy(source.at[part], near.at[part], sems.at[len(copies)])
            )
    return copies


def near_shapes(later):
    return [shape(*far.shape[-2:], far.dtype) for _, far in later]


def fetch_sems(later, more=0):
    return pltpu.SemaphoreType.DMA((max(CHUNKS * len(later) + more, 1),))


def split(x):
    high = x.astype(BF16)
    rest = x - high.astype(F32)
    mid = rest.astype(BF16)
    low = (rest - mid.astype(F32)).astype(BF16)
    return high, mid, low


def split_rows(precision):
    high, mid, low = split(-precision)
    return jnp.concatenate([high, high, high, mid, mid, low], 0)


def split_columns(x):
    high, mid, low = split(x)
    return [high, mid, low, high, mid, high]


def gram_of(x):
    high, mid, low = split(x)
    cross = dot(high, mid, 0, 0) + dot(high, low, 0, 0)
    return (dot(mid, mid, 0, 0) + (cross + cross.T)) + dot(high, high, 0, 0)


def store_packed(ref, gram, total):
    ref[0:HALF, 0:HALF] = gram[0:HALF, 0:HALF]
    ref[0:HALF, HALF:] = gram[HALF:, 0:HALF]
    ref[HALF : HALF + 64, 0:HALF] = gram[HALF : HALF + 64, HALF:]
    ref[HALF : HALF + 64, HALF:] = gram[HALF + 64 :, HALF:]
    ref[HALF + 64 :] = jnp.broadcast_to(total, (PACKED - HALF - 64, RANK))


def gram_kernel(slots, core_ref, mask_ref, u_hbm, w_hbm, *refs):
    sems = refs[-1]
    count = len(slots)
    others, (keep_ref, send_ref, u_ref, w_ref) = refs[:count], refs[count : count + 4]
    nears = refs[count + 4 : -1]
    first = core_ref[0] == 0
    rows = u_ref.shape[0] // 2
    copies = [pltpu.make_async_copy(w_hbm, w_ref, sems.at[0])]
    for j in range(2):
        part = pl.ds(j * rows, rows)
        copies.append(pltpu.make_async_copy(u_hbm.at[part], u_ref.at[part], sems.at[j + 1]))
    copies += fetches(slots, others, nears, sems.at[pl.ds(3, CHUNKS * count)])
    for copy in copies:
        copy.start()
    copies[0].wait()
    item = w_ref[...]
    gram_i = gram_of(item)
    total_i = jnp.sum(item, 0, keepdims=True)
    gram_u, total_u = 0.0, 0.0
    for j in range(2):
        copies[j + 1].wait()
        user = u_ref[j * rows : (j + 1) * rows]
        gram_u += gram_of(user)
        total_u += jnp.sum(user, 0, keepdims=True)
    store_packed(
        keep_ref, jnp.where(first, gram_u, gram_i), jnp.where(first, total_u, total_i)
    )
    store_packed(
        send_ref, jnp.where(first, gram_i, gram_u), jnp.where(first, total_i, total_u)
    )
    for copy in copies[3:]:
        copy.wait()


def grams(core, mask, users, items, later):
    packed = shape(PACKED, RANK)
    slots, fars = zip(*later)
    return call(
        functools.partial(gram_kernel, slots),
        (packed, packed, shape(*users.shape), shape(*items.shape), *near_shapes(later)),
        [SMEM, SMEM, ANY, ANY] + [ANY] * len(later),
        [fetch_sems(later, 3)],
    )(core, mask, users, items, *fars)


def halves_kernel(core_ref, keep_ref, got_ref, mine_ref, send_ref):
    lower = core_ref[1] == 0
    rows = mine_ref.shape[0]
    both = keep_ref[...] + got_ref[...]
    mine_ref[...] = jnp.where(lower, both[:rows], both[rows:])
    send_ref[...] = jnp.where(lower, both[rows:], both[:rows])


def halves(core, keep, got):
    half = shape(PACKED // 2, RANK)
    return call(halves_kernel, (half, half), [SMEM, VMEM, VMEM])(core, keep, got)


def sum_kernel(a_ref, b_ref, out_ref):
    out_ref[...] = a_ref[...] + b_ref[...]


def added(a, b):
    return call(sum_kernel, shape(*a.shape), [VMEM, VMEM])(a, b)


def inverse_factor(x):
    count = HALF // LANES
    tile = (LANES, HALF)
    rows = [x[LANES * q : LANES * (q + 1)] for q in range(count)]
    sub = lax.broadcasted_iota(jnp.int32, tile, 0)
    lane = lax.broadcasted_iota(jnp.int32, tile, 1)
    done = []
    for p in range(count):
        k = LANES * p
        cols = [
            [jnp.broadcast_to(rows[q][:, k + c : k + c + 1], tile) for q in range(p, count)]
            for c in range(LANES)
        ]
        panel = (lane >= k) & (lane < k + LANES)
        rows[p] = jnp.where(panel, jnp.where(lane - k == sub, 1.0, 0.0), rows[p])
        for q in range(p + 1, count):
            rows[q] = jnp.where(panel, 0.0, rows[q])
        scale = jnp.zeros(tile, F32)
        for i in range(LANES):
            pivot = jnp.broadcast_to(cols[i][0][i : i + 1], tile)
            inverse = 1.0 / pivot
            scale = jnp.where(sub == i, pivot, scale)
            factor = [v * inverse for v in cols[i]]
            factor[0] = jnp.where(sub > i, factor[0], 0.0)
            for c in range(i + 1, LANES):
                row = jnp.broadcast_to(cols[c][0][i : i + 1], tile)
                for q in range(count - p):
                    cols[c][q] = cols[c][q] - factor[q] * row
            row = jnp.broadcast_to(rows[p][i : i + 1], tile)
            for q in range(count - p):
                rows[p + q] = rows[p + q] - factor[q] * row
        done.append(jnp.where(lane < k + LANES, rows[p] * lax.rsqrt(scale), 0.0))
    return jnp.concatenate(done, 0)


def draw_kernel(counts, core_ref, mine_ref, other_ref, wu_ref, wi_ref, out_ref):
    first = core_ref[0] == 0
    lower = core_ref[1] == 0
    n = jnp.where(first, counts[0], counts[1])
    mine, other = mine_ref[...], other_ref[...]
    packed = jnp.concatenate(
        [jnp.where(lower, mine, other), jnp.where(lower, other, mine)], 0
    )
    bartlett_top = jnp.where(first, wu_ref[0:HALF], wi_ref[0:HALF])
    bartlett_low = jnp.where(first, wu_ref[HALF:], wi_ref[HALF:])
    mean = packed[HALF + 64 : HALF + 72] / n
    outer = dot(mean * 0.125, mean, 0, 0, HIGHEST)
    factor = n * n / (2.0 + n)
    diag = lax.broadcasted_iota(jnp.int32, (HALF, HALF), 0) == lax.broadcasted_iota(
        jnp.int32, (HALF, HALF), 1
    )
    eye = jnp.where(diag, 1.0, 0.0)
    s11 = eye + packed[0:HALF, 0:HALF] - factor * outer[0:HALF, 0:HALF]
    s21 = packed[0:HALF, HALF:] - factor * outer[HALF:, 0:HALF]
    gram22 = jnp.concatenate(
        [packed[HALF : HALF + 64, 0:HALF], packed[HALF : HALF + 64, HALF:]], 0
    )
    s22 = eye + gram22 - factor * outer[HALF:, HALF:]
    g1 = inverse_factor(s11)
    l21 = dot(s21, g1, 1, 1, HIGHEST)
    s22 = s22 - dot(l21, l21, 1, 1, HIGHEST)
    top = dot(g1, bartlett_top, 0, 0, HIGHEST)
    carry = dot(l21, g1, 1, 0, HIGHEST)
    g2 = inverse_factor(s22)
    low = dot(g2, bartlett_low, 0, 0, HIGHEST)
    top = top - dot(carry, low, 0, 0, HIGHEST)
    both = jnp.concatenate([top, low], 0)
    out_ref[0:RANK] = dot(both, both, 1, 1, HIGHEST)
    out_ref[RANK:] = n * mean / (2.0 + n)


def draw(counts, core, mine, other, wishart_user, wishart_item):
    return call(
        functools.partial(draw_kernel, counts),
        shape(RANK + 8, RANK),
        [SMEM, VMEM, VMEM, VMEM, VMEM],
    )(core, mine, other, wishart_user, wishart_item)


def prior_of(users, core_ref, mine_ref, other_ref):
    take = (core_ref[0] == 0) == users
    precision = jnp.where(take, mine_ref[0:RANK], other_ref[0:RANK])
    center = jnp.where(take, mine_ref[RANK : RANK + 1], other_ref[RANK : RANK + 1])
    return split_rows(precision), center


def residue_into(res_ref, at, ratings_ref, mask_ref, substep, row, rows, low_u, low_w):
    predicted = dot(low_u, low_w, 1, 1)
    for a in range(rows // TILE):
        for j in range(low_w.shape[0] // TILE):
            ra = slice(at + a * TILE, at + (a + 1) * TILE)
            pa = slice(a * TILE, (a + 1) * TILE)
            ij = slice(j * TILE, (j + 1) * TILE)
            seen = mask_ref[substep, j, (row + at) // TILE + a].astype(F32)
            gap = ratings_ref[ra, ij].astype(F32) - predicted[pa, ij]
            res_ref[ra, ij] = (gap * seen).astype(BF16)


def first_kernel(weight, row, slots, noisy, mask_ref, ratings_ref, r_ref, u_ref, w_ref, *refs):
    un_ref, refs = (refs[0], refs[1:]) if noisy else (None, refs)
    count = len(slots)
    fars, (rt_ref, acc_ref) = refs[:count], refs[count : count + 2]
    nears = refs[count + 2 : 2 * count + 2]
    res_ref, low_ref, sems = refs[2 * count + 2 :]
    copies = fetches(slots, fars, nears, sems)
    for copy in copies:
        copy.start()
    low_w = w_ref[...].astype(BF16)
    total = rt_ref.shape[0]
    here = slice(row, row + total)
    low_ref[...] = u_ref[here].astype(BF16)
    rows = 256
    for t in range(total // rows):
        low_u = low_ref[t * rows : (t + 1) * rows]
        residue_into(
            res_ref, t * rows, ratings_ref.at[here], mask_ref, 0, row, rows, low_u, low_w
        )
    acc_ref[...] = dot(low_ref[...], res_ref[...], 0, 0)
    like_u = dot(res_ref[...], low_w, 1, 0)
    if un_ref is None:
        for copy in copies:
            copy.wait()
        un_ref = nears[0]
        copies = []
    rt_ref[...] = (
        DECAY * r_ref[here]
        + RATE * weight * like_u
        + jnp.sqrt(0.4) * un_ref[here].astype(F32)
    )
    for copy in copies:
        copy.wait()


def first_part(weight, row, rows, mask, ratings, user_mom, users, items, noise, later):
    k = users.shape[1]
    ni = items.shape[0]
    slots = tuple(slot for slot, _ in later)
    fars = [far for _, far in later]
    noise = [] if noise is None else [noise]
    rt, acc, *nears = call(
        functools.partial(first_kernel, weight, row, slots, len(noise)),
        (shape(rows, k), shape(k, ni), *near_shapes(later)),
        [SMEM, VMEM, VMEM, VMEM, VMEM] + [VMEM] * len(noise) + [ANY] * len(fars),
        [pltpu.VMEM((rows, ni), BF16), pltpu.VMEM((rows, k), BF16), fetch_sems(later)],
    )(mask, ratings, user_mom, users, items, *noise, *fars)
    return rt, acc, nears


def item_start_kernel(weight, w_ref, q_ref, in_ref, *refs):
    accs, out_ref = refs[:-1], refs[-1]
    like = accs[0][...]
    for acc in accs[1:]:
        like = like + acc[...]
    ni = w_ref.shape[0]
    out_ref[0:ni] = (
        DECAY * q_ref[...] + RATE * weight * like.T + jnp.sqrt(0.4) * in_ref[...].astype(F32)
    )
    out_ref[ni:] = w_ref[...]


def item_start(weight, items, item_mom, item_noise, accs):
    ni, k = item_mom.shape
    return call(
        functools.partial(item_start_kernel, weight),
        shape(2 * ni, k),
        [VMEM] * (3 + len(accs)),
    )(items, item_mom, item_noise, *accs)


def finish_kernel(is_user, pieces, core_ref, mine_ref, other_ref, *refs):
    (x_out, m_out, rhs_ref), ins = refs[-3:], refs[:-3]
    rhs, center = prior_of(is_user, core_ref, mine_ref, other_ref)
    rhs_ref[...] = rhs
    rows = 256
    read = lambda piece, at, size: ins[piece[0]][piece[1] + at : piece[1] + at + size]
    base = 0
    for size, factors, momenta in pieces:
        for at in range(0, size, rows):
            step = min(rows, size - at)
            x = read(factors, at, step)
            columns = jnp.concatenate(split_columns(x - center), 1)
            m = read(momenta, at, step) + RATE * dot(columns, rhs_ref[...], 1, 0)
            m_out[base : base + step] = m
            x_out[base : base + step] = x + RATE * m
            base += step


def finish(is_user, core, mine, other, arrays, pieces):
    n, k = sum(p[0] for p in pieces), arrays[0].shape[1]
    return call(
        functools.partial(finish_kernel, is_user, pieces),
        (shape(n, k), shape(n, k)),
        [SMEM] + [VMEM] * (2 + len(arrays)),
        [pltpu.VMEM((6 * RANK, k), BF16)],
    )(core, mine, other, *arrays)


def items_kernel(
    weight,
    substep,
    mask_ref,
    core_ref,
    mine_ref,
    other_ref,
    ratings_ref,
    u_ref,
    w_ref,
    q_ref,
    in_ref,
    res_ref,
    q_out,
    low_ref,
):
    low_w = w_ref[...].astype(BF16)
    rows = 256
    for t in range(u_ref.shape[0] // rows):
        here = slice(t * rows, (t + 1) * rows)
        low_u = u_ref[here].astype(BF16)
        low_ref[here] = low_u
        residue_into(res_ref, t * rows, ratings_ref, mask_ref, substep, 0, rows, low_u, low_w)
    like = dot(low_ref[...], res_ref[...], 0, 0)
    rhs, center = prior_of(False, core_ref, mine_ref, other_ref)
    prior = dot(jnp.concatenate(split_columns(w_ref[...] - center), 1), rhs, 1, 0)
    q_out[...] = (
        DECAY * q_ref[...]
        + RATE * (weight * like.T + prior)
        + jnp.sqrt(0.4) * in_ref[...].astype(F32)
    )


def items_step(weight, substep, mask, core, mine, other, ratings, users, w, q, item_noise):
    n, k = users.shape
    ni = w.shape[0]
    return call(
        functools.partial(items_kernel, weight, substep),
        (shape(n, ni, BF16), shape(ni, k)),
        [SMEM, SMEM] + [VMEM] * 7,
        [pltpu.VMEM((n, k), BF16)],
    )(mask, core, mine, other, ratings, users, w, q, item_noise)


def users_kernel(
    weight,
    slots,
    core_ref,
    mine_ref,
    other_ref,
    res_ref,
    w_ref,
    u_ref,
    r_ref,
    un_ref,
    *refs,
):
    if slots:
        count = len(slots)
        fars, (u_out, r_out), nears = refs[:count], refs[count : count + 2], refs[count + 2 : -2]
        rhs_ref, sems = refs[-2:]
        copies = fetches(slots, fars, nears, sems)
    else:
        (u_out, r_out, *draws), rhs_ref, copies = refs[:-1], refs[-1], []
    for copy in copies:
        copy.start()
    if not slots:
        mine, other = mine_ref[0:RANK], other_ref[0:RANK]
        first = core_ref[0] == 0
        draws[0][...] = jnp.where(first, mine, other)
        draws[1][...] = jnp.where(first, other, mine)
    ni = w_ref.shape[0]
    rhs_ref[0:ni] = w_ref[...].astype(BF16)
    rhs, center = prior_of(True, core_ref, mine_ref, other_ref)
    rhs_ref[ni:] = rhs
    rows = 256
    for t in range(u_ref.shape[0] // rows):
        here = slice(t * rows, (t + 1) * rows)
        x = u_ref[here]
        columns = jnp.concatenate(split_columns(x - center), 1)
        like = dot(res_ref[here], rhs_ref[0:ni], 1, 0)
        r = (
            DECAY * r_ref[here]
            + RATE * (weight * like + dot(columns, rhs_ref[ni:], 1, 0))
            + jnp.sqrt(0.4) * un_ref[here].astype(F32)
        )
        r_out[here] = r
        u_out[here] = x + RATE * r
    for copy in copies:
        copy.wait()


def users_step(weight, later, core, mine, other, res, w, users, user_mom, user_noise):
    n, k = users.shape
    ni = w.shape[0]
    slots = tuple(slot for slot, _ in later)
    fars = [far for _, far in later]
    more = near_shapes(later) if later else [shape(RANK, RANK)] * 2
    return call(
        functools.partial(users_kernel, weight, slots),
        (shape(n, k), shape(n, k), *more),
        [SMEM] + [VMEM] * 7 + [ANY] * len(fars),
        [pltpu.VMEM((ni + 6 * RANK, k), BF16)] + [fetch_sems(later)] * bool(later),
        near=bool(later),
    )(core, mine, other, res, w, users, user_mom, user_noise, *fars)


def arrived_kernel(w_ref, q_ref, w_out, q_out, sum_ref, sems):
    first = pltpu.make_async_copy(q_ref, q_out, sems.at[0])
    first.start()
    sum_ref[...] = w_ref[...] + RATE * q_ref[...]
    second = pltpu.make_async_copy(sum_ref, w_out, sems.at[1])
    second.start()
    first.wait()
    second.wait()


def arrived(before, came):
    out = pltpu.HBM(came.shape, F32)
    return pl.pallas_call(
        arrived_kernel,
        out_shape=(out, out),
        in_specs=[VMEM, VMEM],
        out_specs=(ANY, ANY),
        scratch_shapes=[pltpu.VMEM(came.shape, F32), pltpu.SemaphoreType.DMA((2,))],
        compiler_params=params(),
        cost_estimate=pl.CostEstimate(flops=1000, bytes_accessed=1000, transcendentals=0),
    )(before, came)


def swapped(array, by, size):
    return lax.ppermute(array, "blk", [(i, i ^ by) for i in range(size)])


def local(
    ratings,
    tile_mask,
    user_factors,
    user_momentum,
    item_factors,
    item_momentum,
    user_noise,
    item_noise,
    wishart_user,
    wishart_item,
):
    blocks = lax.axis_size("blk")
    blk = lax.axis_index("blk")
    user_rows = user_factors.shape[0]
    item_rows = item_factors.shape[0]
    weight = 1.0 * blocks
    back = [(i, (i - 1) % blocks) for i in range(blocks)]
    shift = lambda array: lax.ppermute(array, "blk", back)
    fence = lax.optimization_barrier

    odd = blk % 2
    half = (blk // 2) % 2
    core = jnp.stack([odd, half]).astype(jnp.int32)

    mask = tile_mask.transpose(0, 2, 1)
    parts = 4
    rows = user_rows // parts
    rts, accs, loaded = [], [], []
    later = [
        [(0, user_noise), (None, item_momentum), (0, item_noise)],
        [(1, ratings)],
        [(1, user_noise), (1, item_noise)],
        [(None, wishart_user), (None, wishart_item)],
    ]

    keep, send, near_u, near_w, near_ratings, near_r = grams(
        core,
        mask,
        user_factors,
        item_factors,
        [(0, ratings), (None, user_momentum)],
    )
    got = swapped(send, 1, blocks)
    mine, send = halves(core, keep, got)

    def part():
        j = len(rts)
        rt, acc, nears = first_part(
            weight,
            j * rows,
            rows,
            mask,
            near_ratings,
            near_r,
            near_u,
            near_w,
            loaded[0][0] if j else None,
            later[j],
        )
        rts.append(rt)
        accs.append(acc)
        loaded.append(nears)

    by = 2
    while by < blocks:
        send, near_u = fence((send, near_u))
        got = swapped(send, by, blocks)
        if len(rts) < parts:
            part()
            got, rts[-1], accs[-1] = fence((got, rts[-1], accs[-1]))
        mine = added(mine, got)
        send = mine
        by = by * 2
    send, near_u = fence((send, near_u))
    other = swapped(send, 2, blocks)
    while len(rts) < parts:
        part()
    item_part = item_start(weight, near_w, loaded[0][1], loaded[0][2], accs)
    other, item_part, *rts = fence((other, item_part, *rts))
    early = shift(item_part)
    wu, wi = loaded[3]
    near = {1: (loaded[1][0], *loaded[2])}
    counts = (1.0 * user_rows * blocks, 1.0 * item_rows * blocks)
    drawn = draw(counts, core, mine, other, wu, wi)
    peer = swapped(drawn, 1, blocks)

    users, user_mom = finish(
        True,
        core,
        drawn,
        peer,
        (near_u, *rts),
        tuple((rows, (0, j * rows), (1 + j, 0)) for j in range(parts)),
    )
    items, item_mom = finish(
        False,
        core,
        drawn,
        peer,
        (early,),
        ((item_rows, (0, item_rows), (0, 0)),),
    )
    for substep in range(1, SUBSTEPS):
        last = substep == SUBSTEPS - 1
        here_ratings, here_un, here_in = near[substep]
        later = [] if last else [(substep + 1, x) for x in (ratings, user_noise, item_noise)]
        before = shift(items)
        res, item_next = items_step(
            weight,
            substep,
            mask,
            core,
            drawn,
            peer,
            here_ratings,
            users,
            items,
            item_mom,
            here_in,
        )
        came = shift(item_next)
        users, user_mom, *more = users_step(
            weight, later, core, drawn, peer, res, items, users, user_mom, here_un
        )
        before, users, user_mom, *more = fence((before, users, user_mom, *more))
        if not last:
            near[substep + 1] = more
            items = before + RATE * came
            item_mom = came
    items, item_mom = arrived(before, came)
    return (users, user_mom, items, item_mom, *more)


def solution(mesh):
    placed = (
        P(None, ("chain", "blk"), None),
        P(None, ("chain", "blk"), None),
        P(("chain", "blk"), None),
        P(("chain", "blk"), None),
        P(("chain", "blk"), None),
        P(("chain", "blk"), None),
        P(None, ("chain", "blk"), None),
        P(None, ("chain", "blk"), None),
        P("chain", None),
        P("chain", None),
    )
    return jax.shard_map(
        local,
        mesh=mesh,
        in_specs=placed,
        out_specs=(
            P(("chain", "blk"), None),
            P(("chain", "blk"), None),
            P(("chain", "blk"), None),
            P(("chain", "blk"), None),
            P("chain", None),
            P("chain", None),
        ),
        check_vma=False,
    )
```

```python
import functools

import jax
import jax.numpy as jnp
from jax import lax
from jax.experimental import pallas as pl
from jax.experimental.pallas import tpu as pltpu
from jax.sharding import PartitionSpec as P

TILE = 128
SUBSTEPS = 3
RANK = 256
HALF = 128
LANES = 8
PACKED = 208
RATE = 0.005
DECAY = 0.8
HIGHEST = lax.Precision.HIGHEST
F32 = jnp.float32
BF16 = jnp.bfloat16
VMEM = pl.BlockSpec(memory_space=pltpu.VMEM)
ANY = pl.BlockSpec(memory_space=pl.ANY)
SMEM = pl.BlockSpec(memory_space=pltpu.SMEM)


def parity():
    return lax.rem(lax.axis_index("blk"), 2)


def upper_half():
    return lax.rem(lax.div(lax.axis_index("blk"), 2), 2)


def dot(a, b, ca, cb, precision=None):
    return lax.dot_general(
        a, b, (((ca,), (cb,)), ((), ())), precision=precision, preferred_element_type=F32
    )


def params(mib=16):
    return pltpu.CompilerParams(vmem_limit_bytes=mib << 20)


def shape(rows, columns, dtype=F32):
    return jax.ShapeDtypeStruct((rows, columns), dtype)


def call(kernel, outs, in_specs, scratch=(), near=True, aliases={}):
    cost = pl.CostEstimate(flops=1000, bytes_accessed=1000, transcendentals=0)
    space = (lambda o: pltpu.VMEM(o.shape, o.dtype)) if near else (lambda o: o)
    run = pl.pallas_call(
        kernel,
        out_shape=jax.tree.map(space, outs),
        in_specs=in_specs,
        out_specs=jax.tree.map(lambda _: VMEM, outs),
        scratch_shapes=list(scratch),
        input_output_aliases=aliases,
        compiler_params=params(),
        cost_estimate=cost,
    )

    def placed(*args):
        spaces = {id(ANY): pltpu.HBM, id(VMEM): pltpu.VMEM}
        return run(
            *(
                pltpu.with_memory_space_constraint(a, spaces[id(s)]) if id(s) in spaces else a
                for a, s in zip(args, in_specs)
            )
        )

    return placed


CHUNKS = 4


def fetches(slots, fars, nears, sems):
    copies = []
    for slot, far, near in zip(slots, fars, nears):
        source = far if slot is None else far.at[slot]
        if len(near.shape) > 2:
            copies.append(pltpu.make_async_copy(source, near, sems.at[len(copies)]))
            continue
        rows = near.shape[0] // CHUNKS
        for c in range(CHUNKS):
            part = pl.ds(c * rows, rows)
            copies.append(
                pltpu.make_async_copy(source.at[part], near.at[part], sems.at[len(copies)])
            )
    return copies


def near_shapes(later):
    cut = [far.shape if slot is None else far.shape[1:] for slot, far in later]
    return [jax.ShapeDtypeStruct(c, far.dtype) for c, (_, far) in zip(cut, later)]


def fetch_sems(later, more=0):
    return pltpu.SemaphoreType.DMA((max(CHUNKS * len(later) + more, 1),))


def split(x):
    high = x.astype(BF16)
    rest = x - high.astype(F32)
    mid = rest.astype(BF16)
    low = (rest - mid.astype(F32)).astype(BF16)
    return high, mid, low


def split_rows(precision):
    high, mid, low = split(-precision)
    return jnp.concatenate([high, high, high, mid, mid, low], 0)


def split_columns(x):
    high, mid, low = split(x)
    return [high, mid, low, high, mid, high]


def gram_of(x):
    high, mid, low = split(x)
    cross = dot(high, mid, 0, 0) + dot(high, low, 0, 0)
    return (dot(mid, mid, 0, 0) + (cross + cross.T)) + dot(high, high, 0, 0)


def store_packed(ref, gram, total):
    ref[0:HALF, 0:HALF] = gram[0:HALF, 0:HALF]
    ref[0:HALF, HALF:] = gram[HALF:, 0:HALF]
    ref[HALF : HALF + 64, 0:HALF] = gram[HALF : HALF + 64, HALF:]
    ref[HALF : HALF + 64, HALF:] = gram[HALF + 64 :, HALF:]
    ref[HALF + 64 :] = jnp.broadcast_to(total, (PACKED - HALF - 64, RANK))


def gram_kernel(slots, u_hbm, w_hbm, *refs):
    sems = refs[-1]
    count = len(slots)
    others, (keep_ref, send_ref, u_ref, w_ref) = refs[:count], refs[count : count + 4]
    nears = refs[count + 4 : -1]
    first = parity() == 0
    rows = u_ref.shape[0] // 2
    copies = [pltpu.make_async_copy(w_hbm, w_ref, sems.at[0])]
    for j in range(2):
        part = pl.ds(j * rows, rows)
        copies.append(pltpu.make_async_copy(u_hbm.at[part], u_ref.at[part], sems.at[j + 1]))
    copies += fetches(slots, others, nears, sems.at[pl.ds(3, CHUNKS * count)])
    for copy in copies:
        copy.start()
    copies[0].wait()
    item = w_ref[...]
    gram_i = gram_of(item)
    total_i = jnp.sum(item, 0, keepdims=True)
    gram_u, total_u = 0.0, 0.0
    for j in range(2):
        copies[j + 1].wait()
        user = u_ref[j * rows : (j + 1) * rows]
        gram_u += gram_of(user)
        total_u += jnp.sum(user, 0, keepdims=True)
    store_packed(
        keep_ref, jnp.where(first, gram_u, gram_i), jnp.where(first, total_u, total_i)
    )
    store_packed(
        send_ref, jnp.where(first, gram_i, gram_u), jnp.where(first, total_i, total_u)
    )
    for copy in copies[3:]:
        copy.wait()


def grams(users, items, later):
    packed = shape(PACKED, RANK)
    slots, fars = zip(*later)
    return call(
        functools.partial(gram_kernel, slots),
        (packed, packed, shape(*users.shape), shape(*items.shape), *near_shapes(later)),
        [ANY, ANY] + [ANY] * len(later),
        [fetch_sems(later, 3)],
    )(users, items, *fars)


def halves_kernel(keep_ref, got_ref, mine_ref, send_ref):
    lower = upper_half() == 0
    rows = mine_ref.shape[0]
    both = keep_ref[...] + got_ref[...]
    mine_ref[...] = jnp.where(lower, both[:rows], both[rows:])
    send_ref[...] = jnp.where(lower, both[rows:], both[:rows])


def halves(keep, got):
    half = shape(PACKED // 2, RANK)
    return call(halves_kernel, (half, half), [VMEM, VMEM])(keep, got)


def sum_kernel(a_ref, b_ref, out_ref):
    out_ref[...] = a_ref[...] + b_ref[...]


def added(a, b):
    return call(sum_kernel, shape(*a.shape), [VMEM, VMEM])(a, b)


def inverse_factor(x):
    count = HALF // LANES
    tile = (LANES, HALF)
    rows = [x[LANES * q : LANES * (q + 1)] for q in range(count)]
    sub = lax.broadcasted_iota(jnp.int32, tile, 0)
    lane = lax.broadcasted_iota(jnp.int32, tile, 1)
    done = []
    for p in range(count):
        k = LANES * p
        cols = [
            [jnp.broadcast_to(rows[q][:, k + c : k + c + 1], tile) for q in range(p, count)]
            for c in range(LANES)
        ]
        panel = (lane >= k) & (lane < k + LANES)
        rows[p] = jnp.where(panel, jnp.where(lane - k == sub, 1.0, 0.0), rows[p])
        for q in range(p + 1, count):
            rows[q] = jnp.where(panel, 0.0, rows[q])
        scale = jnp.zeros(tile, F32)
        for i in range(LANES):
            pivot = jnp.broadcast_to(cols[i][0][i : i + 1], tile)
            inverse = 1.0 / pivot
            scale = jnp.where(sub == i, pivot, scale)
            factor = [v * inverse for v in cols[i]]
            factor[0] = jnp.where(sub > i, factor[0], 0.0)
            for c in range(i + 1, LANES):
                row = jnp.broadcast_to(cols[c][0][i : i + 1], tile)
                for q in range(count - p):
                    cols[c][q] = cols[c][q] - factor[q] * row
            row = jnp.broadcast_to(rows[p][i : i + 1], tile)
            for q in range(count - p):
                rows[p + q] = rows[p + q] - factor[q] * row
        done.append(jnp.where(lane < k + LANES, rows[p] * lax.rsqrt(scale), 0.0))
    return jnp.concatenate(done, 0)


def draw_kernel(counts, mine_ref, other_ref, wu_ref, wi_ref, out_ref):
    first = parity() == 0
    lower = upper_half() == 0
    n = jnp.where(first, counts[0], counts[1])
    mine, other = mine_ref[...], other_ref[...]
    packed = jnp.concatenate(
        [jnp.where(lower, mine, other), jnp.where(lower, other, mine)], 0
    )
    bartlett_top = jnp.where(first, wu_ref[0:HALF], wi_ref[0:HALF])
    bartlett_low = jnp.where(first, wu_ref[HALF:], wi_ref[HALF:])
    mean = packed[HALF + 64 : HALF + 72] / n
    outer = dot(mean * 0.125, mean, 0, 0, HIGHEST)
    factor = n * n / (2.0 + n)
    diag = lax.broadcasted_iota(jnp.int32, (HALF, HALF), 0) == lax.broadcasted_iota(
        jnp.int32, (HALF, HALF), 1
    )
    eye = jnp.where(diag, 1.0, 0.0)
    s11 = eye + packed[0:HALF, 0:HALF] - factor * outer[0:HALF, 0:HALF]
    s21 = packed[0:HALF, HALF:] - factor * outer[HALF:, 0:HALF]
    gram22 = jnp.concatenate(
        [packed[HALF : HALF + 64, 0:HALF], packed[HALF : HALF + 64, HALF:]], 0
    )
    s22 = eye + gram22 - factor * outer[HALF:, HALF:]
    g1 = inverse_factor(s11)
    l21 = dot(s21, g1, 1, 1, HIGHEST)
    s22 = s22 - dot(l21, l21, 1, 1, HIGHEST)
    top = dot(g1, bartlett_top, 0, 0, HIGHEST)
    carry = dot(l21, g1, 1, 0, HIGHEST)
    g2 = inverse_factor(s22)
    low = dot(g2, bartlett_low, 0, 0, HIGHEST)
    top = top - dot(carry, low, 0, 0, HIGHEST)
    both = jnp.concatenate([top, low], 0)
    out_ref[0:RANK] = dot(both, both, 1, 1, HIGHEST)
    out_ref[RANK:] = n * mean / (2.0 + n)


def draw(counts, mine, other, wishart_user, wishart_item):
    return call(
        functools.partial(draw_kernel, counts),
        shape(RANK + 8, RANK),
        [VMEM, VMEM, VMEM, VMEM],
    )(mine, other, wishart_user, wishart_item)


def prior_of(users, mine_ref, other_ref):
    take = parity() == (0 if users else 1)
    precision = jnp.where(take, mine_ref[0:RANK], other_ref[0:RANK])
    center = jnp.where(take, mine_ref[RANK : RANK + 1], other_ref[RANK : RANK + 1])
    return split_rows(precision), center


def residue_into(res_ref, at, ratings_ref, mask_ref, substep, row, rows, low_u, low_w):
    predicted = dot(low_u, low_w, 1, 1)
    for a in range(rows // TILE):
        for j in range(low_w.shape[0] // TILE):
            ra = slice(at + a * TILE, at + (a + 1) * TILE)
            pa = slice(a * TILE, (a + 1) * TILE)
            ij = slice(j * TILE, (j + 1) * TILE)
            t = (row + at) // TILE + a
            seen = mask_ref[substep, j : j + 1, t : t + 1].astype(F32)
            gap = ratings_ref[ra, ij].astype(F32) - predicted[pa, ij]
            res_ref[ra, ij] = (gap * seen).astype(BF16)


def first_kernel(weight, row, slots, noisy, mask_ref, ratings_ref, r_ref, u_ref, w_ref, *refs):
    un_ref, refs = (refs[0], refs[1:]) if noisy else (None, refs)
    count = len(slots)
    fars, (rt_ref, acc_ref) = refs[:count], refs[count : count + 2]
    nears = refs[count + 2 : 2 * count + 2]
    res_ref, low_ref, sems = refs[2 * count + 2 :]
    copies = fetches(slots, fars, nears, sems)
    for copy in copies:
        copy.start()
    low_w = w_ref[...].astype(BF16)
    total = rt_ref.shape[0]
    here = slice(row, row + total)
    low_ref[...] = u_ref[here].astype(BF16)
    rows = 256
    for t in range(total // rows):
        low_u = low_ref[t * rows : (t + 1) * rows]
        residue_into(
            res_ref, t * rows, ratings_ref.at[here], mask_ref, 0, row, rows, low_u, low_w
        )
    acc_ref[...] = dot(low_ref[...], res_ref[...], 0, 0)
    like_u = dot(res_ref[...], low_w, 1, 0)
    if un_ref is None:
        for copy in copies:
            copy.wait()
        un_ref = nears[0]
        copies = []
    rt_ref[...] = (
        DECAY * r_ref[here]
        + RATE * weight * like_u
        + jnp.sqrt(0.4) * un_ref[here].astype(F32)
    )
    for copy in copies:
        copy.wait()


def first_part(weight, row, rows, mask, ratings, user_mom, users, items, noise, later):
    k = users.shape[1]
    ni = items.shape[0]
    slots = tuple(slot for slot, _ in later)
    fars = [far for _, far in later]
    noise = [] if noise is None else [noise]
    rt, acc, *nears = call(
        functools.partial(first_kernel, weight, row, slots, len(noise)),
        (shape(rows, k), shape(k, ni), *near_shapes(later)),
        [VMEM] * 5 + [VMEM] * len(noise) + [ANY] * len(fars),
        [pltpu.VMEM((rows, ni), BF16), pltpu.VMEM((rows, k), BF16), fetch_sems(later)],
    )(mask, ratings, user_mom, users, items, *noise, *fars)
    return rt, acc, nears


def item_start_kernel(weight, w_ref, q_ref, in_ref, *refs):
    accs, out_ref = refs[:-1], refs[-1]
    like = accs[0][...]
    for acc in accs[1:]:
        like = like + acc[...]
    ni = w_ref.shape[0]
    out_ref[0:ni] = w_ref[...]
    out_ref[ni:] = (
        DECAY * q_ref[...] + RATE * weight * like.T + jnp.sqrt(0.4) * in_ref[...].astype(F32)
    )


def item_start(weight, items, item_mom, item_noise, accs):
    ni, k = item_mom.shape
    return call(
        functools.partial(item_start_kernel, weight),
        shape(2 * ni, k),
        [VMEM] * (3 + len(accs)),
    )(items, item_mom, item_noise, *accs)


def finish_kernel(mine_ref, other_ref, x_ref, *refs):
    parts, (x_out, m_out, rhs_ref) = refs[:-3], refs[-3:]
    rhs, center = prior_of(True, mine_ref, other_ref)
    rhs_ref[...] = rhs
    rows = 256
    base = 0
    for part in parts:
        for at in range(0, part.shape[0], rows):
            here = slice(base, base + rows)
            x = x_ref[here]
            columns = jnp.concatenate(split_columns(x - center), 1)
            m = part[at : at + rows] + RATE * dot(columns, rhs_ref[...], 1, 0)
            m_out[here] = m
            x_out[here] = x + RATE * m
            base += rows


def finish(mine, other, x, parts):
    n, k = x.shape
    return call(
        finish_kernel,
        (shape(n, k), shape(n, k)),
        [VMEM] * (3 + len(parts)),
        [pltpu.VMEM((6 * RANK, k), BF16)],
    )(mine, other, x, *parts)


def first_items_kernel(mine_ref, other_ref, pack_ref, w_out, q_out):
    rhs, center = prior_of(False, mine_ref, other_ref)
    ni = w_out.shape[0]
    w = pack_ref[0:ni]
    prior = dot(jnp.concatenate(split_columns(w - center), 1), rhs, 1, 0)
    q = pack_ref[ni:] + RATE * prior
    q_out[...] = q
    w_out[...] = w + RATE * q


def first_items(mine, other, pack):
    ni, k = pack.shape[0] // 2, pack.shape[1]
    return call(first_items_kernel, (shape(ni, k),) * 2, [VMEM] * 3)(mine, other, pack)


def items_kernel(weight, substep, turn, mask_ref, mine_ref, other_ref, *refs):
    ratings_ref, u_ref, in_ref, w_ref, q_ref = refs[:5]
    res_ref, out_ref, low_ref, part_ref = refs[-4:]

    def work():
        rhs, center = prior_of(False, mine_ref, other_ref)
        ni = in_ref.shape[0]
        w, q = w_ref[...], q_ref[...]
        if turn is not None:
            w = w + RATE * q
            out_ref[0:ni] = w
        prior = dot(jnp.concatenate(split_columns(w - center), 1), rhs, 1, 0)
        part_ref[...] = DECAY * q + RATE * prior + jnp.sqrt(0.4) * in_ref[...].astype(F32)
        low_w = w.astype(BF16)
        rows = 256
        for t in range(u_ref.shape[0] // rows):
            here = slice(t * rows, (t + 1) * rows)
            low_u = u_ref[here].astype(BF16)
            low_ref[here] = low_u
            residue_into(
                res_ref, t * rows, ratings_ref, mask_ref, substep, 0, rows, low_u, low_w
            )
        like = dot(low_ref[...], res_ref[...], 0, 0)
        out_ref[out_ref.shape[0] - ni :] = part_ref[...] + RATE * weight * like.T

    if turn is None:
        work()
    else:
        pl.when(parity() == turn)(work)


def items_step(weight, substep, turn, mask, mine, other, ratings, users, noise, w, q, res=None):
    n, k = users.shape
    ni = noise.shape[0]
    more = [] if res is None else [res]
    return call(
        functools.partial(items_kernel, weight, substep, turn),
        (shape(n, ni, BF16), shape(ni if turn is None else 2 * ni, k)),
        [VMEM] * (8 + len(more)),
        [pltpu.VMEM((n, k), BF16), pltpu.VMEM((ni, k), F32)],
        aliases={8: 0} if more else {},
    )(mask, mine, other, ratings, users, noise, w, q, *more)


def users_kernel(
    weight,
    slots,
    mine_ref,
    other_ref,
    res_ref,
    u_ref,
    r_ref,
    un_ref,
    even_ref,
    odd_ref,
    *refs,
):
    if slots:
        count = len(slots)
        fars, (u_out, r_out), nears = refs[:count], refs[count : count + 2], refs[count + 2 : -2]
        rhs_ref, sems = refs[-2:]
        copies = fetches(slots, fars, nears, sems)
    else:
        (u_out, r_out, *draws), rhs_ref, copies = refs[:-1], refs[-1], []
    for copy in copies:
        copy.start()
    if not slots:
        mine, other = mine_ref[0:RANK], other_ref[0:RANK]
        first = parity() == 0
        draws[0][...] = jnp.where(first, mine, other)
        draws[1][...] = jnp.where(first, other, mine)
    ni = res_ref.shape[1]
    rhs_ref[0:ni] = jnp.where(parity() == 0, even_ref[0:ni], odd_ref[0:ni]).astype(BF16)
    rhs, center = prior_of(True, mine_ref, other_ref)
    rhs_ref[ni:] = rhs
    rows = 256
    for t in range(u_ref.shape[0] // rows):
        here = slice(t * rows, (t + 1) * rows)
        x = u_ref[here]
        columns = jnp.concatenate(split_columns(x - center), 1)
        like = dot(res_ref[here], rhs_ref[0:ni], 1, 0)
        r = (
            DECAY * r_ref[here]
            + RATE * (weight * like + dot(columns, rhs_ref[ni:], 1, 0))
            + jnp.sqrt(0.4) * un_ref[here].astype(F32)
        )
        r_out[here] = r
        u_out[here] = x + RATE * r
    for copy in copies:
        copy.wait()


def users_step(weight, later, mine, other, res, even, odd, users, user_mom, user_noise):
    n, k = users.shape
    ni = res.shape[1]
    slots = tuple(slot for slot, _ in later)
    fars = [far for _, far in later]
    more = near_shapes(later) if later else [shape(RANK, RANK)] * 2
    return call(
        functools.partial(users_kernel, weight, slots),
        (shape(n, k), shape(n, k), *more),
        [VMEM] * 8 + [ANY] * len(fars),
        [pltpu.VMEM((ni + 6 * RANK, k), BF16)] + [fetch_sems(later)] * bool(later),
        near=bool(later),
    )(mine, other, res, users, user_mom, user_noise, even, odd, *fars)


def arrived_kernel(even_ref, odd_ref, w_out, q_out, w_ref, sems):
    ni = w_ref.shape[0]

    def run(pack_ref):
        first = pltpu.make_async_copy(pack_ref.at[pl.ds(ni, ni)], q_out, sems.at[0])
        first.start()
        w_ref[...] = pack_ref[0:ni] + RATE * pack_ref[ni:]
        second = pltpu.make_async_copy(w_ref, w_out, sems.at[1])
        second.start()
        first.wait()
        second.wait()

    pl.when(parity() == 0)(lambda: run(even_ref))
    pl.when(parity() == 1)(lambda: run(odd_ref))


def arrived(even, odd):
    ni, k = even.shape[0] // 2, even.shape[1]
    out = pltpu.HBM((ni, k), F32)
    near = lambda x: pltpu.with_memory_space_constraint(x, pltpu.VMEM)
    return pl.pallas_call(
        arrived_kernel,
        out_shape=(out, out),
        in_specs=[VMEM, VMEM],
        out_specs=(ANY, ANY),
        scratch_shapes=[pltpu.VMEM((ni, k), F32), pltpu.SemaphoreType.DMA((2,))],
        compiler_params=params(),
        cost_estimate=pl.CostEstimate(flops=1000, bytes_accessed=1000, transcendentals=0),
    )(near(even), near(odd))


def swapped(array, by, size):
    return lax.ppermute(array, "blk", [(i, i ^ by) for i in range(size)])


def local(
    ratings,
    tile_mask,
    user_factors,
    user_momentum,
    item_factors,
    item_momentum,
    user_noise,
    item_noise,
    wishart_user,
    wishart_item,
):
    blocks = lax.axis_size("blk")
    user_rows = user_factors.shape[0]
    item_rows = item_factors.shape[0]
    weight = 1.0 * blocks
    fence = lax.optimization_barrier
    inside = [(i, i - 1) for i in range(1, blocks, 2)]
    across = [(i, (i - 1) % blocks) for i in range(0, blocks, 2)]

    mask = tile_mask.transpose(0, 2, 1)
    parts = 4
    rows = user_rows // parts
    rts, accs, loaded = [], [], []
    later = [
        [(0, user_noise), (None, item_momentum), (0, item_noise)],
        [(1, ratings)],
        [(1, user_noise), (1, item_noise)],
        [(None, wishart_user), (None, wishart_item)],
    ]

    keep, send, near_u, near_w, near_ratings, near_r, mask = grams(
        user_factors,
        item_factors,
        [(0, ratings), (None, user_momentum), (None, mask)],
    )
    got = swapped(send, 1, blocks)
    mine, send = halves(keep, got)

    def part():
        j = len(rts)
        rt, acc, nears = first_part(
            weight,
            j * rows,
            rows,
            mask,
            near_ratings,
            near_r,
            near_u,
            near_w,
            loaded[0][0] if j else None,
            later[j],
        )
        rts.append(rt)
        accs.append(acc)
        loaded.append(nears)

    by = 2
    while by < blocks:
        send, near_u = fence((send, near_u))
        got = swapped(send, by, blocks)
        if len(rts) < parts:
            part()
            got, rts[-1], accs[-1] = fence((got, rts[-1], accs[-1]))
        mine = added(mine, got)
        send = mine
        by = by * 2
    send, near_u = fence((send, near_u))
    other = swapped(send, 2, blocks)
    while len(rts) < parts:
        part()
    item_part = item_start(weight, near_w, loaded[0][1], loaded[0][2], accs)
    other, item_part, *rts = fence((other, item_part, *rts))
    send = lambda array, pairs: lax.ppermute(array, "blk", pairs)
    early = send(item_part, inside + across)
    wu, wi = loaded[3]
    near = (loaded[1][0], *loaded[2])
    counts = (1.0 * user_rows * blocks, 1.0 * item_rows * blocks)
    drawn = draw(counts, mine, other, wu, wi)
    peer = swapped(drawn, 1, blocks)
    users, user_mom = finish(drawn, peer, near_u, rts)
    users, early = fence((users, early))
    items, item_mom = first_items(drawn, peer, early)

    before = send(items, inside + across)
    args = (mask, drawn, peer, near[0], users, near[2])
    res, item_mom = items_step(weight, 1, None, *args, items, item_mom)
    q_even, q_odd = send(item_mom, inside), send(item_mom, across)
    later = [(2, x) for x in (ratings, user_noise, item_noise)]
    users, user_mom, *near = users_step(
        weight, later, drawn, peer, res, items, items, users, user_mom, near[1]
    )
    before, users, user_mom, *near = fence((before, users, user_mom, *near))

    args = (mask, drawn, peer, near[0], users, near[2])
    res, even = items_step(weight, 2, 0, *args, before, q_even)
    pack_odd = send(even, across)
    res, odd = items_step(weight, 2, 1, *args, before, q_odd, res)
    pack_even = send(odd, inside)
    users, user_mom, *precisions = users_step(
        weight, [], drawn, peer, res, even, odd, users, user_mom, near[1]
    )
    pack_odd, users, user_mom, *precisions = fence((pack_odd, users, user_mom, *precisions))
    items, item_mom = arrived(pack_even, pack_odd)
    return (users, user_mom, items, item_mom, *precisions)


def solution(mesh):
    placed = (
        P(None, ("chain", "blk"), None),
        P(None, ("chain", "blk"), None),
        P(("chain", "blk"), None),
        P(("chain", "blk"), None),
        P(("chain", "blk"), None),
        P(("chain", "blk"), None),
        P(None, ("chain", "blk"), None),
        P(None, ("chain", "blk"), None),
        P("chain", None),
        P("chain", None),
    )
    return jax.shard_map(
        local,
        mesh=mesh,
        in_specs=placed,
        out_specs=(
            P(("chain", "blk"), None),
            P(("chain", "blk"), None),
            P(("chain", "blk"), None),
            P(("chain", "blk"), None),
            P("chain", None),
            P("chain", None),
        ),
        check_vma=False,
    )
```

```python
import functools

import jax
import jax.numpy as jnp
from jax import lax
from jax.experimental import pallas as pl
from jax.experimental.pallas import tpu as pltpu
from jax.sharding import PartitionSpec as P

TILE = 128
SUBSTEPS = 3
RANK = 256
HALF = 128
LANES = 8
PACKED = 144
RATE = 0.005
DECAY = 0.8
HIGHEST = lax.Precision.HIGHEST
F32 = jnp.float32
BF16 = jnp.bfloat16
VMEM = pl.BlockSpec(memory_space=pltpu.VMEM)
ANY = pl.BlockSpec(memory_space=pl.ANY)
SMEM = pl.BlockSpec(memory_space=pltpu.SMEM)


def parity():
    return lax.rem(lax.axis_index("blk"), 2)


def upper_half():
    return lax.rem(lax.div(lax.axis_index("blk"), 2), 2)


def dot(a, b, ca, cb, precision=None):
    return lax.dot_general(
        a, b, (((ca,), (cb,)), ((), ())), precision=precision, preferred_element_type=F32
    )


def params(mib=16):
    return pltpu.CompilerParams(vmem_limit_bytes=mib << 20)


def shape(rows, columns, dtype=F32):
    return jax.ShapeDtypeStruct((rows, columns), dtype)


def call(kernel, outs, in_specs, scratch=(), near=True, aliases={}):
    cost = pl.CostEstimate(flops=1000, bytes_accessed=1000, transcendentals=0)
    space = (lambda o: pltpu.VMEM(o.shape, o.dtype)) if near else (lambda o: o)
    run = pl.pallas_call(
        kernel,
        out_shape=jax.tree.map(space, outs),
        in_specs=in_specs,
        out_specs=jax.tree.map(lambda _: VMEM, outs),
        scratch_shapes=list(scratch),
        input_output_aliases=aliases,
        compiler_params=params(),
        cost_estimate=cost,
    )

    def placed(*args):
        spaces = {id(ANY): pltpu.HBM, id(VMEM): pltpu.VMEM}
        return run(
            *(
                pltpu.with_memory_space_constraint(a, spaces[id(s)]) if id(s) in spaces else a
                for a, s in zip(args, in_specs)
            )
        )

    return placed


CHUNKS = 4


def fetches(slots, fars, nears, sems):
    copies = []
    for slot, far, near in zip(slots, fars, nears):
        source = far if slot is None else far.at[slot]
        if len(near.shape) > 2:
            copies.append(pltpu.make_async_copy(source, near, sems.at[len(copies)]))
            continue
        rows = near.shape[0] // CHUNKS
        for c in range(CHUNKS):
            part = pl.ds(c * rows, rows)
            copies.append(
                pltpu.make_async_copy(source.at[part], near.at[part], sems.at[len(copies)])
            )
    return copies


def near_shapes(later):
    cut = [far.shape if slot is None else far.shape[1:] for slot, far in later]
    return [jax.ShapeDtypeStruct(c, far.dtype) for c, (_, far) in zip(cut, later)]


def fetch_sems(later, more=0):
    return pltpu.SemaphoreType.DMA((max(CHUNKS * len(later) + more, 1),))


def split(x):
    high = x.astype(BF16)
    rest = x - high.astype(F32)
    mid = rest.astype(BF16)
    low = (rest - mid.astype(F32)).astype(BF16)
    return high, mid, low


def split_rows(precision):
    high, mid, low = split(-precision)
    return jnp.concatenate([high, high, high, mid, mid, low], 0)


def split_columns(x):
    high, mid, low = split(x)
    return [high, mid, low, high, mid, high]


def gram_of(x):
    high, mid, low = split(x)
    cross = dot(high, mid, 0, 0) + dot(high, low, 0, 0)
    return (dot(mid, mid, 0, 0) + (cross + cross.T)) + dot(high, high, 0, 0)


def corner():
    row = lax.broadcasted_iota(jnp.int32, (HALF, HALF), 0)
    column = lax.broadcasted_iota(jnp.int32, (HALF, HALF), 1)
    return column >= row, column == row


def store_packed(ref, gram, total):
    upper, diagonal = corner()
    last = gram[HALF:, HALF:]
    ref[0:HALF, 0:HALF] = jnp.where(upper, gram[0:HALF, 0:HALF], last)
    ref[0:HALF, HALF:] = gram[0:HALF, HALF:]
    ref[HALF : HALF + 8] = jnp.broadcast_to(total, (8, RANK))
    line = jnp.sum(jnp.where(diagonal, last, 0.0), 0, keepdims=True)
    ref[HALF + 8 :] = jnp.concatenate([jnp.broadcast_to(line, (8, HALF))] * 2, 1)


def gram_kernel(slots, u_hbm, w_hbm, *refs):
    sems = refs[-1]
    count = len(slots)
    others, (keep_ref, send_ref, u_ref, w_ref) = refs[:count], refs[count : count + 4]
    nears = refs[count + 4 : -1]
    first = parity() == 0
    rows = u_ref.shape[0] // 2
    copies = [pltpu.make_async_copy(w_hbm, w_ref, sems.at[0])]
    for j in range(2):
        part = pl.ds(j * rows, rows)
        copies.append(pltpu.make_async_copy(u_hbm.at[part], u_ref.at[part], sems.at[j + 1]))
    copies += fetches(slots, others, nears, sems.at[pl.ds(3, CHUNKS * count)])
    for copy in copies:
        copy.start()
    copies[0].wait()
    item = w_ref[...]
    gram_i = gram_of(item)
    total_i = jnp.sum(item, 0, keepdims=True)
    gram_u, total_u = 0.0, 0.0
    for j in range(2):
        copies[j + 1].wait()
        user = u_ref[j * rows : (j + 1) * rows]
        gram_u += gram_of(user)
        total_u += jnp.sum(user, 0, keepdims=True)
    store_packed(
        keep_ref, jnp.where(first, gram_u, gram_i), jnp.where(first, total_u, total_i)
    )
    store_packed(
        send_ref, jnp.where(first, gram_i, gram_u), jnp.where(first, total_i, total_u)
    )
    for copy in copies[3:]:
        copy.wait()


def grams(users, items, later):
    packed = shape(PACKED, RANK)
    slots, fars = zip(*later)
    return call(
        functools.partial(gram_kernel, slots),
        (packed, packed, shape(*users.shape), shape(*items.shape), *near_shapes(later)),
        [ANY, ANY] + [ANY] * len(later),
        [fetch_sems(later, 3)],
    )(users, items, *fars)


def halves_kernel(keep_ref, got_ref, mine_ref, send_ref):
    lower = upper_half() == 0
    rows = mine_ref.shape[0]
    both = keep_ref[...] + got_ref[...]
    mine_ref[...] = jnp.where(lower, both[:rows], both[rows:])
    send_ref[...] = jnp.where(lower, both[rows:], both[:rows])


def halves(keep, got):
    half = shape(PACKED // 2, RANK)
    return call(halves_kernel, (half, half), [VMEM, VMEM])(keep, got)


def sum_kernel(a_ref, b_ref, out_ref):
    out_ref[...] = a_ref[...] + b_ref[...]


def added(a, b):
    return call(sum_kernel, shape(*a.shape), [VMEM, VMEM])(a, b)


def inverse_factor(x):
    count = HALF // LANES
    tile = (LANES, HALF)
    rows = [x[LANES * q : LANES * (q + 1)] for q in range(count)]
    sub = lax.broadcasted_iota(jnp.int32, tile, 0)
    lane = lax.broadcasted_iota(jnp.int32, tile, 1)
    done = []
    for p in range(count):
        k = LANES * p
        cols = [
            [jnp.broadcast_to(rows[q][:, k + c : k + c + 1], tile) for q in range(p, count)]
            for c in range(LANES)
        ]
        panel = (lane >= k) & (lane < k + LANES)
        rows[p] = jnp.where(panel, jnp.where(lane - k == sub, 1.0, 0.0), rows[p])
        for q in range(p + 1, count):
            rows[q] = jnp.where(panel, 0.0, rows[q])
        scale = jnp.zeros(tile, F32)
        for i in range(LANES):
            pivot = jnp.broadcast_to(cols[i][0][i : i + 1], tile)
            inverse = 1.0 / pivot
            scale = jnp.where(sub == i, pivot, scale)
            factor = [v * inverse for v in cols[i]]
            factor[0] = jnp.where(sub > i, factor[0], 0.0)
            for c in range(i + 1, LANES):
                row = jnp.broadcast_to(cols[c][0][i : i + 1], tile)
                for q in range(count - p):
                    cols[c][q] = cols[c][q] - factor[q] * row
            row = jnp.broadcast_to(rows[p][i : i + 1], tile)
            for q in range(count - p):
                rows[p + q] = rows[p + q] - factor[q] * row
        done.append(jnp.where(lane < k + LANES, rows[p] * lax.rsqrt(scale), 0.0))
    return jnp.concatenate(done, 0)


def draw_kernel(counts, mine_ref, other_ref, wu_ref, wi_ref, out_ref):
    first = parity() == 0
    lower = upper_half() == 0
    n = jnp.where(first, counts[0], counts[1])
    mine, other = mine_ref[...], other_ref[...]
    packed = jnp.concatenate(
        [jnp.where(lower, mine, other), jnp.where(lower, other, mine)], 0
    )
    bartlett_top = jnp.where(first, wu_ref[0:HALF], wi_ref[0:HALF])
    bartlett_low = jnp.where(first, wu_ref[HALF:], wi_ref[HALF:])
    mean = packed[HALF : HALF + 8] / n
    outer = dot(mean * 0.125, mean, 0, 0, HIGHEST)
    factor = n * n / (2.0 + n)
    upper, diagonal = corner()
    eye = jnp.where(diagonal, 1.0, 0.0)
    mixed = packed[0:HALF, 0:HALF]
    above = jnp.where(upper & ~diagonal, mixed, 0.0)
    below = jnp.where(upper, 0.0, mixed)
    line = jnp.broadcast_to(packed[HALF + 8 : HALF + 9, 0:HALF], (HALF, HALF))
    gram11 = jnp.where(upper, mixed, above.T)
    gram22 = jnp.where(diagonal, line, below + below.T)
    s11 = eye + gram11 - factor * outer[0:HALF, 0:HALF]
    s21 = packed[0:HALF, HALF:].T - factor * outer[HALF:, 0:HALF]
    s22 = eye + gram22 - factor * outer[HALF:, HALF:]
    g1 = inverse_factor(s11)
    l21 = dot(s21, g1, 1, 1, HIGHEST)
    s22 = s22 - dot(l21, l21, 1, 1, HIGHEST)
    top = dot(g1, bartlett_top, 0, 0, HIGHEST)
    carry = dot(l21, g1, 1, 0, HIGHEST)
    g2 = inverse_factor(s22)
    low = dot(g2, bartlett_low, 0, 0, HIGHEST)
    top = top - dot(carry, low, 0, 0, HIGHEST)
    both = jnp.concatenate([top, low], 0)
    out_ref[0:RANK] = dot(both, both, 1, 1, HIGHEST)
    out_ref[RANK:] = n * mean / (2.0 + n)


def draw(counts, mine, other, wishart_user, wishart_item):
    return call(
        functools.partial(draw_kernel, counts),
        shape(RANK + 8, RANK),
        [VMEM, VMEM, VMEM, VMEM],
    )(mine, other, wishart_user, wishart_item)


def prior_of(users, mine_ref, other_ref):
    take = parity() == (0 if users else 1)
    precision = jnp.where(take, mine_ref[0:RANK], other_ref[0:RANK])
    center = jnp.where(take, mine_ref[RANK : RANK + 1], other_ref[RANK : RANK + 1])
    return split_rows(precision), center


def residue_into(res_ref, at, ratings_ref, mask_ref, substep, row, rows, low_u, low_w):
    predicted = dot(low_u, low_w, 1, 1)
    for a in range(rows // TILE):
        for j in range(low_w.shape[0] // TILE):
            ra = slice(at + a * TILE, at + (a + 1) * TILE)
            pa = slice(a * TILE, (a + 1) * TILE)
            ij = slice(j * TILE, (j + 1) * TILE)
            t = (row + at) // TILE + a
            seen = mask_ref[substep, j : j + 1, t : t + 1].astype(F32)
            gap = ratings_ref[ra, ij].astype(F32) - predicted[pa, ij]
            res_ref[ra, ij] = (gap * seen).astype(BF16)


def first_kernel(weight, row, slots, noisy, mask_ref, ratings_ref, r_ref, u_ref, w_ref, *refs):
    un_ref, refs = (refs[0], refs[1:]) if noisy else (None, refs)
    count = len(slots)
    fars, (rt_ref, acc_ref) = refs[:count], refs[count : count + 2]
    nears = refs[count + 2 : 2 * count + 2]
    res_ref, low_ref, sems = refs[2 * count + 2 :]
    copies = fetches(slots, fars, nears, sems)
    for copy in copies:
        copy.start()
    low_w = w_ref[...].astype(BF16)
    total = rt_ref.shape[0]
    here = slice(row, row + total)
    low_ref[...] = u_ref[here].astype(BF16)
    rows = 256
    for t in range(total // rows):
        low_u = low_ref[t * rows : (t + 1) * rows]
        residue_into(
            res_ref, t * rows, ratings_ref.at[here], mask_ref, 0, row, rows, low_u, low_w
        )
    acc_ref[...] = dot(low_ref[...], res_ref[...], 0, 0)
    like_u = dot(res_ref[...], low_w, 1, 0)
    if un_ref is None:
        for copy in copies:
            copy.wait()
        un_ref = nears[0]
        copies = []
    rt_ref[...] = (
        DECAY * r_ref[here]
        + RATE * weight * like_u
        + jnp.sqrt(0.4) * un_ref[here].astype(F32)
    )
    for copy in copies:
        copy.wait()


def first_part(weight, row, rows, mask, ratings, user_mom, users, items, noise, later):
    k = users.shape[1]
    ni = items.shape[0]
    slots = tuple(slot for slot, _ in later)
    fars = [far for _, far in later]
    noise = [] if noise is None else [noise]
    rt, acc, *nears = call(
        functools.partial(first_kernel, weight, row, slots, len(noise)),
        (shape(rows, k), shape(k, ni), *near_shapes(later)),
        [VMEM] * 5 + [VMEM] * len(noise) + [ANY] * len(fars),
        [pltpu.VMEM((rows, ni), BF16), pltpu.VMEM((rows, k), BF16), fetch_sems(later)],
    )(mask, ratings, user_mom, users, items, *noise, *fars)
    return rt, acc, nears


def item_start_kernel(weight, w_ref, q_ref, in_ref, *refs):
    accs, out_ref = refs[:-1], refs[-1]
    like = accs[0][...]
    for acc in accs[1:]:
        like = like + acc[...]
    ni = w_ref.shape[0]
    out_ref[0:ni] = w_ref[...]
    out_ref[ni:] = (
        DECAY * q_ref[...] + RATE * weight * like.T + jnp.sqrt(0.4) * in_ref[...].astype(F32)
    )


def item_start(weight, items, item_mom, item_noise, accs):
    ni, k = item_mom.shape
    return call(
        functools.partial(item_start_kernel, weight),
        shape(2 * ni, k),
        [VMEM] * (3 + len(accs)),
    )(items, item_mom, item_noise, *accs)


def finish_kernel(mine_ref, other_ref, x_ref, *refs):
    parts, (x_out, m_out, rhs_ref) = refs[:-3], refs[-3:]
    rhs, center = prior_of(True, mine_ref, other_ref)
    rhs_ref[...] = rhs
    rows = 256
    base = 0
    for part in parts:
        for at in range(0, part.shape[0], rows):
            here = slice(base, base + rows)
            x = x_ref[here]
            columns = jnp.concatenate(split_columns(x - center), 1)
            m = part[at : at + rows] + RATE * dot(columns, rhs_ref[...], 1, 0)
            m_out[here] = m
            x_out[here] = x + RATE * m
            base += rows


def finish(mine, other, x, parts):
    n, k = x.shape
    return call(
        finish_kernel,
        (shape(n, k), shape(n, k)),
        [VMEM] * (3 + len(parts)),
        [pltpu.VMEM((6 * RANK, k), BF16)],
    )(mine, other, x, *parts)


def first_items_kernel(mine_ref, other_ref, pack_ref, w_out, q_out):
    rhs, center = prior_of(False, mine_ref, other_ref)
    ni = w_out.shape[0]
    w = pack_ref[0:ni]
    prior = dot(jnp.concatenate(split_columns(w - center), 1), rhs, 1, 0)
    q = pack_ref[ni:] + RATE * prior
    q_out[...] = q
    w_out[...] = w + RATE * q


def first_items(mine, other, pack):
    ni, k = pack.shape[0] // 2, pack.shape[1]
    return call(first_items_kernel, (shape(ni, k),) * 2, [VMEM] * 3)(mine, other, pack)


def items_kernel(weight, substep, turn, mask_ref, mine_ref, other_ref, *refs):
    ratings_ref, u_ref, in_ref, w_ref, q_ref = refs[:5]
    res_ref, out_ref, low_ref, part_ref = refs[-4:]

    def work():
        rhs, center = prior_of(False, mine_ref, other_ref)
        ni = in_ref.shape[0]
        w, q = w_ref[...], q_ref[...]
        if turn is not None:
            w = w + RATE * q
            out_ref[0:ni] = w
        prior = dot(jnp.concatenate(split_columns(w - center), 1), rhs, 1, 0)
        part_ref[...] = DECAY * q + RATE * prior + jnp.sqrt(0.4) * in_ref[...].astype(F32)
        low_w = w.astype(BF16)
        rows = 256
        for t in range(u_ref.shape[0] // rows):
            here = slice(t * rows, (t + 1) * rows)
            low_u = u_ref[here].astype(BF16)
            low_ref[here] = low_u
            residue_into(
                res_ref, t * rows, ratings_ref, mask_ref, substep, 0, rows, low_u, low_w
            )
        like = dot(low_ref[...], res_ref[...], 0, 0)
        out_ref[out_ref.shape[0] - ni :] = part_ref[...] + RATE * weight * like.T

    if turn is None:
        work()
    else:
        pl.when(parity() == turn)(work)


def items_step(weight, substep, turn, mask, mine, other, ratings, users, noise, w, q, res=None):
    n, k = users.shape
    ni = noise.shape[0]
    more = [] if res is None else [res]
    return call(
        functools.partial(items_kernel, weight, substep, turn),
        (shape(n, ni, BF16), shape(ni if turn is None else 2 * ni, k)),
        [VMEM] * (8 + len(more)),
        [pltpu.VMEM((n, k), BF16), pltpu.VMEM((ni, k), F32)],
        aliases={8: 0} if more else {},
    )(mask, mine, other, ratings, users, noise, w, q, *more)


def users_kernel(
    weight,
    slots,
    mine_ref,
    other_ref,
    res_ref,
    u_ref,
    r_ref,
    un_ref,
    even_ref,
    odd_ref,
    *refs,
):
    if slots:
        count = len(slots)
        fars, (u_out, r_out), nears = refs[:count], refs[count : count + 2], refs[count + 2 : -2]
        rhs_ref, sems = refs[-2:]
        copies = fetches(slots, fars, nears, sems)
    else:
        (u_out, r_out, *draws), rhs_ref, copies = refs[:-1], refs[-1], []
    for copy in copies:
        copy.start()
    if not slots:
        mine, other = mine_ref[0:RANK], other_ref[0:RANK]
        first = parity() == 0
        draws[0][...] = jnp.where(first, mine, other)
        draws[1][...] = jnp.where(first, other, mine)
    ni = res_ref.shape[1]
    rhs_ref[0:ni] = jnp.where(parity() == 0, even_ref[0:ni], odd_ref[0:ni]).astype(BF16)
    rhs, center = prior_of(True, mine_ref, other_ref)
    rhs_ref[ni:] = rhs
    rows = 256
    for t in range(u_ref.shape[0] // rows):
        here = slice(t * rows, (t + 1) * rows)
        x = u_ref[here]
        columns = jnp.concatenate(split_columns(x - center), 1)
        like = dot(res_ref[here], rhs_ref[0:ni], 1, 0)
        r = (
            DECAY * r_ref[here]
            + RATE * (weight * like + dot(columns, rhs_ref[ni:], 1, 0))
            + jnp.sqrt(0.4) * un_ref[here].astype(F32)
        )
        r_out[here] = r
        u_out[here] = x + RATE * r
    for copy in copies:
        copy.wait()


def users_step(weight, later, mine, other, res, even, odd, users, user_mom, user_noise):
    n, k = users.shape
    ni = res.shape[1]
    slots = tuple(slot for slot, _ in later)
    fars = [far for _, far in later]
    more = near_shapes(later) if later else [shape(RANK, RANK)] * 2
    return call(
        functools.partial(users_kernel, weight, slots),
        (shape(n, k), shape(n, k), *more),
        [VMEM] * 8 + [ANY] * len(fars),
        [pltpu.VMEM((ni + 6 * RANK, k), BF16)] + [fetch_sems(later)] * bool(later),
        near=bool(later),
    )(mine, other, res, users, user_mom, user_noise, even, odd, *fars)


def arrived_kernel(even_ref, odd_ref, w_out, q_out, w_ref, sems):
    ni = w_ref.shape[0]

    def run(pack_ref):
        first = pltpu.make_async_copy(pack_ref.at[pl.ds(ni, ni)], q_out, sems.at[0])
        first.start()
        w_ref[...] = pack_ref[0:ni] + RATE * pack_ref[ni:]
        second = pltpu.make_async_copy(w_ref, w_out, sems.at[1])
        second.start()
        first.wait()
        second.wait()

    pl.when(parity() == 0)(lambda: run(even_ref))
    pl.when(parity() == 1)(lambda: run(odd_ref))


def arrived(even, odd):
    ni, k = even.shape[0] // 2, even.shape[1]
    out = pltpu.HBM((ni, k), F32)
    near = lambda x: pltpu.with_memory_space_constraint(x, pltpu.VMEM)
    return pl.pallas_call(
        arrived_kernel,
        out_shape=(out, out),
        in_specs=[VMEM, VMEM],
        out_specs=(ANY, ANY),
        scratch_shapes=[pltpu.VMEM((ni, k), F32), pltpu.SemaphoreType.DMA((2,))],
        compiler_params=params(),
        cost_estimate=pl.CostEstimate(flops=1000, bytes_accessed=1000, transcendentals=0),
    )(near(even), near(odd))


def swapped(array, by, size):
    return lax.ppermute(array, "blk", [(i, i ^ by) for i in range(size)])


def local(
    ratings,
    tile_mask,
    user_factors,
    user_momentum,
    item_factors,
    item_momentum,
    user_noise,
    item_noise,
    wishart_user,
    wishart_item,
):
    blocks = lax.axis_size("blk")
    user_rows = user_factors.shape[0]
    item_rows = item_factors.shape[0]
    weight = 1.0 * blocks
    fence = lax.optimization_barrier
    inside = [(i, i - 1) for i in range(1, blocks, 2)]
    across = [(i, (i - 1) % blocks) for i in range(0, blocks, 2)]

    mask = tile_mask.transpose(0, 2, 1)
    parts = 4
    rows = user_rows // parts
    rts, accs, loaded = [], [], []
    later = [
        [(0, user_noise), (None, item_momentum), (0, item_noise)],
        [(1, ratings)],
        [(1, user_noise), (1, item_noise)],
        [(None, wishart_user), (None, wishart_item)],
    ]

    keep, send, near_u, near_w, near_ratings, near_r, mask = grams(
        user_factors,
        item_factors,
        [(0, ratings), (None, user_momentum), (None, mask)],
    )
    got = swapped(send, 1, blocks)
    mine, send = halves(keep, got)

    def part():
        j = len(rts)
        rt, acc, nears = first_part(
            weight,
            j * rows,
            rows,
            mask,
            near_ratings,
            near_r,
            near_u,
            near_w,
            loaded[0][0] if j else None,
            later[j],
        )
        rts.append(rt)
        accs.append(acc)
        loaded.append(nears)

    by = 2
    while by < blocks:
        send, near_u = fence((send, near_u))
        got = swapped(send, by, blocks)
        if len(rts) < parts:
            part()
            got, rts[-1], accs[-1] = fence((got, rts[-1], accs[-1]))
        mine = added(mine, got)
        send = mine
        by = by * 2
    send, near_u = fence((send, near_u))
    other = swapped(send, 2, blocks)
    while len(rts) < parts:
        part()
    item_part = item_start(weight, near_w, loaded[0][1], loaded[0][2], accs)
    other, item_part, *rts = fence((other, item_part, *rts))
    send = lambda array, pairs: lax.ppermute(array, "blk", pairs)
    early = send(item_part, inside + across)
    wu, wi = loaded[3]
    near = (loaded[1][0], *loaded[2])
    counts = (1.0 * user_rows * blocks, 1.0 * item_rows * blocks)
    drawn = draw(counts, mine, other, wu, wi)
    peer = swapped(drawn, 1, blocks)
    users, user_mom = finish(drawn, peer, near_u, rts)
    users, early = fence((users, early))
    items, item_mom = first_items(drawn, peer, early)

    before = send(items, inside + across)
    args = (mask, drawn, peer, near[0], users, near[2])
    res, item_mom = items_step(weight, 1, None, *args, items, item_mom)
    q_even, q_odd = send(item_mom, inside), send(item_mom, across)
    later = [(2, x) for x in (ratings, user_noise, item_noise)]
    users, user_mom, *near = users_step(
        weight, later, drawn, peer, res, items, items, users, user_mom, near[1]
    )
    before, users, user_mom, *near = fence((before, users, user_mom, *near))

    args = (mask, drawn, peer, near[0], users, near[2])
    res, even = items_step(weight, 2, 0, *args, before, q_even)
    pack_odd = send(even, across)
    res, odd = items_step(weight, 2, 1, *args, before, q_odd, res)
    pack_even = send(odd, inside)
    users, user_mom, *precisions = users_step(
        weight, [], drawn, peer, res, even, odd, users, user_mom, near[1]
    )
    pack_odd, users, user_mom, *precisions = fence((pack_odd, users, user_mom, *precisions))
    items, item_mom = arrived(pack_even, pack_odd)
    return (users, user_mom, items, item_mom, *precisions)


def solution(mesh):
    placed = (
        P(None, ("chain", "blk"), None),
        P(None, ("chain", "blk"), None),
        P(("chain", "blk"), None),
        P(("chain", "blk"), None),
        P(("chain", "blk"), None),
        P(("chain", "blk"), None),
        P(None, ("chain", "blk"), None),
        P(None, ("chain", "blk"), None),
        P("chain", None),
        P("chain", None),
    )
    return jax.shard_map(
        local,
        mesh=mesh,
        in_specs=placed,
        out_specs=(
            P(("chain", "blk"), None),
            P(("chain", "blk"), None),
            P(("chain", "blk"), None),
            P(("chain", "blk"), None),
            P("chain", None),
            P("chain", None),
        ),
        check_vma=False,
    )
```

```python
import functools

import jax
import jax.numpy as jnp
from jax import lax
from jax.experimental import pallas as pl
from jax.experimental.pallas import tpu as pltpu
from jax.sharding import PartitionSpec as P

TILE = 128
SUBSTEPS = 3
RANK = 256
HALF = 128
LANES = 8
PACKED = 144
RATE = 0.005
DECAY = 0.8
HIGHEST = lax.Precision.HIGHEST
F32 = jnp.float32
BF16 = jnp.bfloat16
VMEM = pl.BlockSpec(memory_space=pltpu.VMEM)
ANY = pl.BlockSpec(memory_space=pl.ANY)
SMEM = pl.BlockSpec(memory_space=pltpu.SMEM)


def parity():
    return lax.rem(lax.axis_index("blk"), 2)


def upper_half():
    return lax.rem(lax.div(lax.axis_index("blk"), 2), 2)


def dot(a, b, ca, cb, precision=None):
    return lax.dot_general(
        a, b, (((ca,), (cb,)), ((), ())), precision=precision, preferred_element_type=F32
    )


def params(mib=16):
    return pltpu.CompilerParams(vmem_limit_bytes=mib << 20)


def shape(rows, columns, dtype=F32):
    return jax.ShapeDtypeStruct((rows, columns), dtype)


def call(kernel, outs, in_specs, scratch=(), near=True, aliases={}):
    cost = pl.CostEstimate(flops=1000, bytes_accessed=1000, transcendentals=0)
    space = (lambda o: pltpu.VMEM(o.shape, o.dtype)) if near else (lambda o: o)
    run = pl.pallas_call(
        kernel,
        out_shape=jax.tree.map(space, outs),
        in_specs=in_specs,
        out_specs=jax.tree.map(lambda _: VMEM, outs),
        scratch_shapes=list(scratch),
        input_output_aliases=aliases,
        compiler_params=params(),
        cost_estimate=cost,
    )

    def placed(*args):
        spaces = {id(ANY): pltpu.HBM, id(VMEM): pltpu.VMEM}
        return run(
            *(
                pltpu.with_memory_space_constraint(a, spaces[id(s)]) if id(s) in spaces else a
                for a, s in zip(args, in_specs)
            )
        )

    return placed


CHUNKS = 4


def fetches(slots, fars, nears, sems):
    copies = []
    for slot, far, near in zip(slots, fars, nears):
        source = far if slot is None else far.at[slot]
        if len(near.shape) > 2:
            copies.append(pltpu.make_async_copy(source, near, sems.at[len(copies)]))
            continue
        rows = near.shape[0] // CHUNKS
        for c in range(CHUNKS):
            part = pl.ds(c * rows, rows)
            copies.append(
                pltpu.make_async_copy(source.at[part], near.at[part], sems.at[len(copies)])
            )
    return copies


def near_shapes(later):
    cut = [far.shape if slot is None else far.shape[1:] for slot, far in later]
    return [jax.ShapeDtypeStruct(c, far.dtype) for c, (_, far) in zip(cut, later)]


def fetch_sems(later, more=0):
    return pltpu.SemaphoreType.DMA((max(CHUNKS * len(later) + more, 1),))


def split(x):
    high = x.astype(BF16)
    rest = x - high.astype(F32)
    mid = rest.astype(BF16)
    low = (rest - mid.astype(F32)).astype(BF16)
    return high, mid, low


def split_rows(precision):
    high, mid, low = split(-precision)
    return jnp.concatenate([high, high, high, mid, mid, low], 0)


def split_columns(x):
    high, mid, low = split(x)
    return [high, mid, low, high, mid, high]


def gram_of(x):
    high, mid, low = split(x)
    cross = dot(high, mid, 0, 0) + dot(high, low, 0, 0)
    return (dot(mid, mid, 0, 0) + (cross + cross.T)) + dot(high, high, 0, 0)


def corner():
    row = lax.broadcasted_iota(jnp.int32, (HALF, HALF), 0)
    column = lax.broadcasted_iota(jnp.int32, (HALF, HALF), 1)
    return column >= row, column == row


def store_packed(ref, gram, total):
    upper, diagonal = corner()
    last = gram[HALF:, HALF:]
    ref[0:HALF, 0:HALF] = jnp.where(upper, gram[0:HALF, 0:HALF], last)
    ref[0:HALF, HALF:] = gram[0:HALF, HALF:]
    ref[HALF : HALF + 8] = jnp.broadcast_to(total, (8, RANK))
    line = jnp.sum(jnp.where(diagonal, last, 0.0), 0, keepdims=True)
    ref[HALF + 8 :] = jnp.concatenate([jnp.broadcast_to(line, (8, HALF))] * 2, 1)


def gram_kernel(slots, u_hbm, w_hbm, *refs):
    sems = refs[-1]
    count = len(slots)
    others, (keep_ref, send_ref, u_ref, w_ref) = refs[:count], refs[count : count + 4]
    nears = refs[count + 4 : -1]
    first = parity() == 0
    rows = u_ref.shape[0] // 2
    copies = [pltpu.make_async_copy(w_hbm, w_ref, sems.at[0])]
    for j in range(2):
        part = pl.ds(j * rows, rows)
        copies.append(pltpu.make_async_copy(u_hbm.at[part], u_ref.at[part], sems.at[j + 1]))
    copies += fetches(slots, others, nears, sems.at[pl.ds(3, CHUNKS * count)])
    for copy in copies:
        copy.start()
    copies[0].wait()
    item = w_ref[...]
    gram_i = gram_of(item)
    total_i = jnp.sum(item, 0, keepdims=True)
    gram_u, total_u = 0.0, 0.0
    for j in range(2):
        copies[j + 1].wait()
        user = u_ref[j * rows : (j + 1) * rows]
        gram_u += gram_of(user)
        total_u += jnp.sum(user, 0, keepdims=True)
    store_packed(
        keep_ref, jnp.where(first, gram_u, gram_i), jnp.where(first, total_u, total_i)
    )
    store_packed(
        send_ref, jnp.where(first, gram_i, gram_u), jnp.where(first, total_i, total_u)
    )
    for copy in copies[3:]:
        copy.wait()


def grams(users, items, later):
    packed = shape(PACKED, RANK)
    slots, fars = zip(*later)
    return call(
        functools.partial(gram_kernel, slots),
        (packed, packed, shape(*users.shape), shape(*items.shape), *near_shapes(later)),
        [ANY, ANY] + [ANY] * len(later),
        [fetch_sems(later, 3)],
    )(users, items, *fars)


def halves_kernel(keep_ref, got_ref, mine_ref, send_ref):
    lower = upper_half() == 0
    rows = mine_ref.shape[0]
    both = keep_ref[...] + got_ref[...]
    mine_ref[...] = jnp.where(lower, both[:rows], both[rows:])
    send_ref[...] = jnp.where(lower, both[rows:], both[:rows])


def halves(keep, got):
    half = shape(PACKED // 2, RANK)
    return call(halves_kernel, (half, half), [VMEM, VMEM])(keep, got)


def sum_kernel(a_ref, b_ref, out_ref):
    out_ref[...] = a_ref[...] + b_ref[...]


def added(a, b):
    return call(sum_kernel, shape(*a.shape), [VMEM, VMEM])(a, b)


def inverse_factor(x):
    count = HALF // LANES
    tile = (LANES, HALF)
    rows = [x[LANES * q : LANES * (q + 1)] for q in range(count)]
    sub = lax.broadcasted_iota(jnp.int32, tile, 0)
    lane = lax.broadcasted_iota(jnp.int32, tile, 1)
    done = []
    for p in range(count):
        k = LANES * p
        cols = [
            [jnp.broadcast_to(rows[q][:, k + c : k + c + 1], tile) for q in range(p, count)]
            for c in range(LANES)
        ]
        panel = (lane >= k) & (lane < k + LANES)
        rows[p] = jnp.where(panel, jnp.where(lane - k == sub, 1.0, 0.0), rows[p])
        for q in range(p + 1, count):
            rows[q] = jnp.where(panel, 0.0, rows[q])
        scale = jnp.zeros(tile, F32)
        for i in range(LANES):
            pivot = jnp.broadcast_to(cols[i][0][i : i + 1], tile)
            inverse = 1.0 / pivot
            scale = jnp.where(sub == i, pivot, scale)
            factor = [v * inverse for v in cols[i]]
            factor[0] = jnp.where(sub > i, factor[0], 0.0)
            for c in range(i + 1, LANES):
                row = jnp.broadcast_to(cols[c][0][i : i + 1], tile)
                for q in range(count - p):
                    cols[c][q] = cols[c][q] - factor[q] * row
            row = jnp.broadcast_to(rows[p][i : i + 1], tile)
            for q in range(count - p):
                rows[p + q] = rows[p + q] - factor[q] * row
        done.append(jnp.where(lane < k + LANES, rows[p] * lax.rsqrt(scale), 0.0))
    return jnp.concatenate(done, 0)


def draw_kernel(counts, mine_ref, other_ref, wu_ref, wi_ref, out_ref):
    first = parity() == 0
    lower = upper_half() == 0
    n = jnp.where(first, counts[0], counts[1])
    mine, other = mine_ref[...], other_ref[...]
    packed = jnp.concatenate(
        [jnp.where(lower, mine, other), jnp.where(lower, other, mine)], 0
    )
    bartlett_top = jnp.where(first, wu_ref[0:HALF], wi_ref[0:HALF])
    bartlett_low = jnp.where(first, wu_ref[HALF:], wi_ref[HALF:])
    mean = packed[HALF : HALF + 8] / n
    outer = dot(mean * 0.125, mean, 0, 0, HIGHEST)
    factor = n * n / (2.0 + n)
    upper, diagonal = corner()
    eye = jnp.where(diagonal, 1.0, 0.0)
    mixed = packed[0:HALF, 0:HALF]
    above = jnp.where(upper & ~diagonal, mixed, 0.0)
    below = jnp.where(upper, 0.0, mixed)
    line = jnp.broadcast_to(packed[HALF + 8 : HALF + 9, 0:HALF], (HALF, HALF))
    gram11 = jnp.where(upper, mixed, above.T)
    gram22 = jnp.where(diagonal, line, below + below.T)
    s11 = eye + gram11 - factor * outer[0:HALF, 0:HALF]
    s21 = packed[0:HALF, HALF:].T - factor * outer[HALF:, 0:HALF]
    s22 = eye + gram22 - factor * outer[HALF:, HALF:]
    g1 = inverse_factor(s11)
    l21 = dot(s21, g1, 1, 1, HIGHEST)
    s22 = s22 - dot(l21, l21, 1, 1, HIGHEST)
    top = dot(g1, bartlett_top, 0, 0, HIGHEST)
    carry = dot(l21, g1, 1, 0, HIGHEST)
    g2 = inverse_factor(s22)
    low = dot(g2, bartlett_low, 0, 0, HIGHEST)
    top = top - dot(carry, low, 0, 0, HIGHEST)
    both = jnp.concatenate([top, low], 0)
    out_ref[0:RANK] = dot(both, both, 1, 1, HIGHEST)
    out_ref[RANK:] = n * mean / (2.0 + n)


def draw(counts, mine, other, wishart_user, wishart_item):
    return call(
        functools.partial(draw_kernel, counts),
        shape(RANK + 8, RANK),
        [VMEM, VMEM, VMEM, VMEM],
    )(mine, other, wishart_user, wishart_item)


def prior_of(users, mine_ref, other_ref):
    take = parity() == (0 if users else 1)
    precision = jnp.where(take, mine_ref[0:RANK], other_ref[0:RANK])
    center = jnp.where(take, mine_ref[RANK : RANK + 1], other_ref[RANK : RANK + 1])
    return split_rows(precision), center


def residue_into(res_ref, at, ratings_ref, mask_ref, substep, row, rows, low_u, low_w):
    predicted = dot(low_u, low_w, 1, 1)
    for a in range(rows // TILE):
        for j in range(low_w.shape[0] // TILE):
            ra = slice(at + a * TILE, at + (a + 1) * TILE)
            pa = slice(a * TILE, (a + 1) * TILE)
            ij = slice(j * TILE, (j + 1) * TILE)
            t = (row + at) // TILE + a
            seen = mask_ref[substep, j : j + 1, t : t + 1].astype(F32)
            gap = ratings_ref[ra, ij].astype(F32) - predicted[pa, ij]
            res_ref[ra, ij] = (gap * seen).astype(BF16)


def first_kernel(weight, row, slots, noisy, mask_ref, ratings_ref, r_ref, u_ref, w_ref, *refs):
    un_ref, refs = (refs[0], refs[1:]) if noisy else (None, refs)
    count = len(slots)
    fars, (rt_ref, acc_ref) = refs[:count], refs[count : count + 2]
    nears = refs[count + 2 : 2 * count + 2]
    res_ref, low_ref, sems = refs[2 * count + 2 :]
    copies = fetches(slots, fars, nears, sems)
    for copy in copies:
        copy.start()
    low_w = w_ref[...].astype(BF16)
    total = rt_ref.shape[0]
    here = slice(row, row + total)
    low_ref[...] = u_ref[here].astype(BF16)
    rows = 256
    for t in range(total // rows):
        low_u = low_ref[t * rows : (t + 1) * rows]
        residue_into(
            res_ref, t * rows, ratings_ref.at[here], mask_ref, 0, row, rows, low_u, low_w
        )
    acc_ref[...] = dot(low_ref[...], res_ref[...], 0, 0)
    like_u = dot(res_ref[...], low_w, 1, 0)
    if un_ref is None:
        for copy in copies:
            copy.wait()
        un_ref = nears[0]
        copies = []
    rt_ref[...] = (
        DECAY * r_ref[here]
        + RATE * weight * like_u
        + jnp.sqrt(0.4) * un_ref[here].astype(F32)
    )
    for copy in copies:
        copy.wait()


def first_part(weight, row, rows, mask, ratings, user_mom, users, items, noise, later):
    k = users.shape[1]
    ni = items.shape[0]
    slots = tuple(slot for slot, _ in later)
    fars = [far for _, far in later]
    noise = [] if noise is None else [noise]
    rt, acc, *nears = call(
        functools.partial(first_kernel, weight, row, slots, len(noise)),
        (shape(rows, k), shape(k, ni), *near_shapes(later)),
        [VMEM] * 5 + [VMEM] * len(noise) + [ANY] * len(fars),
        [pltpu.VMEM((rows, ni), BF16), pltpu.VMEM((rows, k), BF16), fetch_sems(later)],
    )(mask, ratings, user_mom, users, items, *noise, *fars)
    return rt, acc, nears


def item_start_kernel(weight, w_ref, q_ref, in_ref, *refs):
    accs, out_ref = refs[:-1], refs[-1]
    like = accs[0][...]
    for acc in accs[1:]:
        like = like + acc[...]
    ni = w_ref.shape[0]
    out_ref[0:ni] = w_ref[...]
    out_ref[ni:] = (
        DECAY * q_ref[...] + RATE * weight * like.T + jnp.sqrt(0.4) * in_ref[...].astype(F32)
    )


def item_start(weight, items, item_mom, item_noise, accs):
    ni, k = item_mom.shape
    return call(
        functools.partial(item_start_kernel, weight),
        shape(2 * ni, k),
        [VMEM] * (3 + len(accs)),
    )(items, item_mom, item_noise, *accs)


def finish_kernel(mine_ref, other_ref, x_ref, *refs):
    parts, (x_out, m_out, rhs_ref) = refs[:-3], refs[-3:]
    rhs, center = prior_of(True, mine_ref, other_ref)
    rhs_ref[...] = rhs
    rows = 256
    base = 0
    for part in parts:
        for at in range(0, part.shape[0], rows):
            here = slice(base, base + rows)
            x = x_ref[here]
            columns = jnp.concatenate(split_columns(x - center), 1)
            m = part[at : at + rows] + RATE * dot(columns, rhs_ref[...], 1, 0)
            m_out[here] = m
            x_out[here] = x + RATE * m
            base += rows


def finish(mine, other, x, parts):
    n, k = x.shape
    return call(
        finish_kernel,
        (shape(n, k), shape(n, k)),
        [VMEM] * (3 + len(parts)),
        [pltpu.VMEM((6 * RANK, k), BF16)],
    )(mine, other, x, *parts)


def first_items_kernel(mine_ref, other_ref, pack_ref, w_out, q_out):
    rhs, center = prior_of(False, mine_ref, other_ref)
    ni = w_out.shape[0]
    w = pack_ref[0:ni]
    prior = dot(jnp.concatenate(split_columns(w - center), 1), rhs, 1, 0)
    q = pack_ref[ni:] + RATE * prior
    q_out[...] = q
    w_out[...] = w + RATE * q


def first_items(mine, other, pack):
    ni, k = pack.shape[0] // 2, pack.shape[1]
    return call(first_items_kernel, (shape(ni, k),) * 2, [VMEM] * 3)(mine, other, pack)


def items_kernel(weight, substep, turn, mask_ref, mine_ref, other_ref, *refs):
    ratings_ref, u_ref, in_ref, w_ref, q_ref = refs[:5]
    res_ref, out_ref, low_ref, part_ref = refs[-4:]

    def work():
        rhs, center = prior_of(False, mine_ref, other_ref)
        ni = in_ref.shape[0]
        w, q = w_ref[...], q_ref[...]
        if turn is not None:
            w = w + RATE * q
            out_ref[0:ni] = w
        prior = dot(jnp.concatenate(split_columns(w - center), 1), rhs, 1, 0)
        part_ref[...] = DECAY * q + RATE * prior + jnp.sqrt(0.4) * in_ref[...].astype(F32)
        low_w = w.astype(BF16)
        rows = 256
        for t in range(u_ref.shape[0] // rows):
            here = slice(t * rows, (t + 1) * rows)
            low_u = u_ref[here].astype(BF16)
            low_ref[here] = low_u
            residue_into(
                res_ref, t * rows, ratings_ref, mask_ref, substep, 0, rows, low_u, low_w
            )
        like = dot(low_ref[...], res_ref[...], 0, 0)
        out_ref[out_ref.shape[0] - ni :] = part_ref[...] + RATE * weight * like.T

    if turn is None:
        work()
    else:
        pl.when(parity() == turn)(work)


def items_step(weight, substep, turn, mask, mine, other, ratings, users, noise, w, q, res=None):
    n, k = users.shape
    ni = noise.shape[0]
    more = [] if res is None else [res]
    return call(
        functools.partial(items_kernel, weight, substep, turn),
        (shape(n, ni, BF16), shape(ni if turn is None else 2 * ni, k)),
        [VMEM] * (8 + len(more)),
        [pltpu.VMEM((n, k), BF16), pltpu.VMEM((ni, k), F32)],
        aliases={8: 0} if more else {},
    )(mask, mine, other, ratings, users, noise, w, q, *more)


def users_kernel(
    weight,
    slots,
    mine_ref,
    other_ref,
    res_ref,
    u_ref,
    r_ref,
    un_ref,
    even_ref,
    odd_ref,
    *refs,
):
    if slots:
        count = len(slots)
        fars, (u_out, r_out), nears = refs[:count], refs[count : count + 2], refs[count + 2 : -2]
        rhs_ref, sems = refs[-2:]
        copies = fetches(slots, fars, nears, sems)
    else:
        (u_out, r_out, *draws), rhs_ref, copies = refs[:-1], refs[-1], []
    for copy in copies:
        copy.start()
    if not slots:
        mine, other = mine_ref[0:RANK], other_ref[0:RANK]
        first = parity() == 0
        draws[0][...] = jnp.where(first, mine, other)
        draws[1][...] = jnp.where(first, other, mine)
    ni = res_ref.shape[1]
    rhs_ref[0:ni] = jnp.where(parity() == 0, even_ref[0:ni], odd_ref[0:ni]).astype(BF16)
    rhs, center = prior_of(True, mine_ref, other_ref)
    rhs_ref[ni:] = rhs
    rows = 256
    for t in range(u_ref.shape[0] // rows):
        here = slice(t * rows, (t + 1) * rows)
        x = u_ref[here]
        columns = jnp.concatenate(split_columns(x - center), 1)
        like = dot(res_ref[here], rhs_ref[0:ni], 1, 0)
        r = (
            DECAY * r_ref[here]
            + RATE * (weight * like + dot(columns, rhs_ref[ni:], 1, 0))
            + jnp.sqrt(0.4) * un_ref[here].astype(F32)
        )
        r_out[here] = r
        u_out[here] = x + RATE * r
    for copy in copies:
        copy.wait()


def users_step(weight, later, mine, other, res, even, odd, users, user_mom, user_noise):
    n, k = users.shape
    ni = res.shape[1]
    slots = tuple(slot for slot, _ in later)
    fars = [far for _, far in later]
    more = near_shapes(later) if later else [shape(RANK, RANK)] * 2
    return call(
        functools.partial(users_kernel, weight, slots),
        (shape(n, k), shape(n, k), *more),
        [VMEM] * 8 + [ANY] * len(fars),
        [pltpu.VMEM((ni + 6 * RANK, k), BF16)] + [fetch_sems(later)] * bool(later),
        near=bool(later),
    )(mine, other, res, users, user_mom, user_noise, even, odd, *fars)


def arrived_kernel(even_ref, odd_ref, w_out, q_out, w_ref, sems):
    ni = w_ref.shape[0]

    def run(pack_ref):
        first = pltpu.make_async_copy(pack_ref.at[pl.ds(ni, ni)], q_out, sems.at[0])
        first.start()
        w_ref[...] = pack_ref[0:ni] + RATE * pack_ref[ni:]
        second = pltpu.make_async_copy(w_ref, w_out, sems.at[1])
        second.start()
        first.wait()
        second.wait()

    pl.when(parity() == 0)(lambda: run(even_ref))
    pl.when(parity() == 1)(lambda: run(odd_ref))


def arrived(even, odd):
    ni, k = even.shape[0] // 2, even.shape[1]
    out = pltpu.HBM((ni, k), F32)
    near = lambda x: pltpu.with_memory_space_constraint(x, pltpu.VMEM)
    return pl.pallas_call(
        arrived_kernel,
        out_shape=(out, out),
        in_specs=[VMEM, VMEM],
        out_specs=(ANY, ANY),
        scratch_shapes=[pltpu.VMEM((ni, k), F32), pltpu.SemaphoreType.DMA((2,))],
        compiler_params=params(),
        cost_estimate=pl.CostEstimate(flops=1000, bytes_accessed=1000, transcendentals=0),
    )(near(even), near(odd))


def swapped(array, by, size):
    return lax.ppermute(array, "blk", [(i, i ^ by) for i in range(size)])


def local(
    ratings,
    tile_mask,
    user_factors,
    user_momentum,
    item_factors,
    item_momentum,
    user_noise,
    item_noise,
    wishart_user,
    wishart_item,
):
    blocks = lax.axis_size("blk")
    user_rows = user_factors.shape[0]
    item_rows = item_factors.shape[0]
    weight = 1.0 * blocks
    fence = lax.optimization_barrier
    inside = [(i, i ^ 1) for i in range(blocks)]
    across = [(i, (i - 1) % blocks) for i in range(0, blocks, 2)]
    ring = [(i, (i - 1) % blocks) for i in range(blocks)]

    mask = tile_mask.transpose(0, 2, 1)
    parts = 4
    rows = user_rows // parts
    rts, accs, loaded = [], [], []
    later = [
        [(0, user_noise), (None, item_momentum), (0, item_noise)],
        [(1, ratings)],
        [(1, user_noise), (1, item_noise)],
        [(None, wishart_user), (None, wishart_item)],
    ]

    keep, send, near_u, near_w, near_ratings, near_r, mask = grams(
        user_factors,
        item_factors,
        [(0, ratings), (None, user_momentum), (None, mask)],
    )
    got = swapped(send, 1, blocks)
    mine, send = halves(keep, got)

    def part():
        j = len(rts)
        rt, acc, nears = first_part(
            weight,
            j * rows,
            rows,
            mask,
            near_ratings,
            near_r,
            near_u,
            near_w,
            loaded[0][0] if j else None,
            later[j],
        )
        rts.append(rt)
        accs.append(acc)
        loaded.append(nears)

    by = 2
    while by < blocks:
        send, near_u = fence((send, near_u))
        got = swapped(send, by, blocks)
        if len(rts) < parts:
            part()
            got, rts[-1], accs[-1] = fence((got, rts[-1], accs[-1]))
        mine = added(mine, got)
        send = mine
        by = by * 2
    send, near_u = fence((send, near_u))
    other = swapped(send, 2, blocks)
    while len(rts) < parts:
        part()
    item_part = item_start(weight, near_w, loaded[0][1], loaded[0][2], accs)
    other, item_part, *rts = fence((other, item_part, *rts))
    send = lambda array, pairs: lax.ppermute(array, "blk", pairs)
    early = send(item_part, ring)
    wu, wi = loaded[3]
    near = (loaded[1][0], *loaded[2])
    counts = (1.0 * user_rows * blocks, 1.0 * item_rows * blocks)
    drawn = draw(counts, mine, other, wu, wi)
    peer = swapped(drawn, 1, blocks)
    users, user_mom = finish(drawn, peer, near_u, rts)
    users, early = fence((users, early))
    items, item_mom = first_items(drawn, peer, early)

    before = send(items, ring)
    args = (mask, drawn, peer, near[0], users, near[2])
    res, item_mom = items_step(weight, 1, None, *args, items, item_mom)
    q_even, q_odd = send(item_mom, inside), send(item_mom, across)
    later = [(2, x) for x in (ratings, user_noise, item_noise)]
    users, user_mom, *near = users_step(
        weight, later, drawn, peer, res, items, items, users, user_mom, near[1]
    )
    before, users, user_mom, *near = fence((before, users, user_mom, *near))

    args = (mask, drawn, peer, near[0], users, near[2])
    res, even = items_step(weight, 2, 0, *args, before, q_even)
    pack_odd = send(even, across)
    res, odd = items_step(weight, 2, 1, *args, before, q_odd, res)
    pack_even = send(odd, inside)
    users, user_mom, *precisions = users_step(
        weight, [], drawn, peer, res, even, odd, users, user_mom, near[1]
    )
    pack_odd, users, user_mom, *precisions = fence((pack_odd, users, user_mom, *precisions))
    items, item_mom = arrived(pack_even, pack_odd)
    return (users, user_mom, items, item_mom, *precisions)


def solution(mesh):
    placed = (
        P(None, ("chain", "blk"), None),
        P(None, ("chain", "blk"), None),
        P(("chain", "blk"), None),
        P(("chain", "blk"), None),
        P(("chain", "blk"), None),
        P(("chain", "blk"), None),
        P(None, ("chain", "blk"), None),
        P(None, ("chain", "blk"), None),
        P("chain", None),
        P("chain", None),
    )
    return jax.shard_map(
        local,
        mesh=mesh,
        in_specs=placed,
        out_specs=(
            P(("chain", "blk"), None),
            P(("chain", "blk"), None),
            P(("chain", "blk"), None),
            P(("chain", "blk"), None),
            P("chain", None),
            P("chain", None),
        ),
        check_vma=False,
    )
```

```python
import functools

import jax
import jax.numpy as jnp
from jax import lax
from jax.experimental import pallas as pl
from jax.experimental.pallas import tpu as pltpu
from jax.sharding import PartitionSpec as P

TILE = 128
SUBSTEPS = 3
RANK = 256
HALF = 128
LANES = 8
PACKED = 144
RATE = 0.005
DECAY = 0.8
HIGHEST = lax.Precision.HIGHEST
F32 = jnp.float32
BF16 = jnp.bfloat16
VMEM = pl.BlockSpec(memory_space=pltpu.VMEM)
ANY = pl.BlockSpec(memory_space=pl.ANY)
SMEM = pl.BlockSpec(memory_space=pltpu.SMEM)


def parity():
    return lax.rem(lax.axis_index("blk"), 2)


def upper_half():
    return lax.rem(lax.div(lax.axis_index("blk"), 2), 2)


def dot(a, b, ca, cb, precision=None):
    return lax.dot_general(
        a, b, (((ca,), (cb,)), ((), ())), precision=precision, preferred_element_type=F32
    )


def params(mib=16):
    return pltpu.CompilerParams(vmem_limit_bytes=mib << 20)


def shape(rows, columns, dtype=F32):
    return jax.ShapeDtypeStruct((rows, columns), dtype)


def call(kernel, outs, in_specs, scratch=(), near=True, aliases={}):
    cost = pl.CostEstimate(flops=1000, bytes_accessed=1000, transcendentals=0)
    space = (lambda o: pltpu.VMEM(o.shape, o.dtype)) if near else (lambda o: o)
    run = pl.pallas_call(
        kernel,
        out_shape=jax.tree.map(space, outs),
        in_specs=in_specs,
        out_specs=jax.tree.map(lambda _: VMEM, outs),
        scratch_shapes=list(scratch),
        input_output_aliases=aliases,
        compiler_params=params(),
        cost_estimate=cost,
    )

    def placed(*args):
        spaces = {id(ANY): pltpu.HBM, id(VMEM): pltpu.VMEM}
        return run(
            *(
                pltpu.with_memory_space_constraint(a, spaces[id(s)]) if id(s) in spaces else a
                for a, s in zip(args, in_specs)
            )
        )

    return placed


CHUNKS = 4


def fetches(slots, fars, nears, sems):
    copies = []
    for slot, far, near in zip(slots, fars, nears):
        source = far if slot is None else far.at[slot]
        if len(near.shape) > 2:
            copies.append(pltpu.make_async_copy(source, near, sems.at[len(copies)]))
            continue
        rows = near.shape[0] // CHUNKS
        for c in range(CHUNKS):
            part = pl.ds(c * rows, rows)
            copies.append(
                pltpu.make_async_copy(source.at[part], near.at[part], sems.at[len(copies)])
            )
    return copies


def near_shapes(later):
    cut = [far.shape if slot is None else far.shape[1:] for slot, far in later]
    return [jax.ShapeDtypeStruct(c, far.dtype) for c, (_, far) in zip(cut, later)]


def fetch_sems(later, more=0):
    return pltpu.SemaphoreType.DMA((max(CHUNKS * len(later) + more, 1),))


def split(x):
    high = x.astype(BF16)
    rest = x - high.astype(F32)
    mid = rest.astype(BF16)
    low = (rest - mid.astype(F32)).astype(BF16)
    return high, mid, low


def split_rows(precision):
    high, mid, low = split(-precision)
    return jnp.concatenate([high, high, high, mid, mid, low], 0)


def split_columns(x):
    high, mid, low = split(x)
    return [high, mid, low, high, mid, high]


def gram_of(x):
    high, mid, low = split(x)
    cross = dot(high, mid, 0, 0) + dot(high, low, 0, 0)
    return (dot(mid, mid, 0, 0) + (cross + cross.T)) + dot(high, high, 0, 0)


def corner():
    row = lax.broadcasted_iota(jnp.int32, (HALF, HALF), 0)
    column = lax.broadcasted_iota(jnp.int32, (HALF, HALF), 1)
    return column >= row, column == row


def store_packed(ref, gram, total):
    upper, diagonal = corner()
    last = gram[HALF:, HALF:]
    ref[0:HALF, 0:HALF] = jnp.where(upper, gram[0:HALF, 0:HALF], last)
    ref[0:HALF, HALF:] = gram[0:HALF, HALF:]
    ref[HALF : HALF + 8] = jnp.broadcast_to(total, (8, RANK))
    line = jnp.sum(jnp.where(diagonal, last, 0.0), 0, keepdims=True)
    ref[HALF + 8 :] = jnp.concatenate([jnp.broadcast_to(line, (8, HALF))] * 2, 1)


def gram_kernel(slots, u_hbm, w_hbm, *refs):
    sems = refs[-1]
    count = len(slots)
    others, (keep_ref, send_ref, u_ref, w_ref) = refs[:count], refs[count : count + 4]
    nears = refs[count + 4 : -1]
    first = parity() == 0
    copies = [
        pltpu.make_async_copy(w_hbm, w_ref, sems.at[0]),
        pltpu.make_async_copy(u_hbm, u_ref, sems.at[1]),
    ]
    copies += fetches(slots, others, nears, sems.at[pl.ds(2, CHUNKS * count)])
    for copy in copies:
        copy.start()
    copies[0].wait()
    item = w_ref[...]
    gram_i = gram_of(item)
    total_i = jnp.sum(item, 0, keepdims=True)
    copies[1].wait()
    user = u_ref[...]
    gram_u = gram_of(user)
    total_u = jnp.sum(user, 0, keepdims=True)
    store_packed(
        keep_ref, jnp.where(first, gram_u, gram_i), jnp.where(first, total_u, total_i)
    )
    store_packed(
        send_ref, jnp.where(first, gram_i, gram_u), jnp.where(first, total_i, total_u)
    )
    for copy in copies[2:]:
        copy.wait()


def grams(users, items, later):
    packed = shape(PACKED, RANK)
    slots, fars = zip(*later)
    return call(
        functools.partial(gram_kernel, slots),
        (packed, packed, shape(*users.shape), shape(*items.shape), *near_shapes(later)),
        [ANY, ANY] + [ANY] * len(later),
        [fetch_sems(later, 2)],
    )(users, items, *fars)


def halves_kernel(keep_ref, got_ref, mine_ref, send_ref):
    lower = upper_half() == 0
    rows = mine_ref.shape[0]
    both = keep_ref[...] + got_ref[...]
    mine_ref[...] = jnp.where(lower, both[:rows], both[rows:])
    send_ref[...] = jnp.where(lower, both[rows:], both[:rows])


def halves(keep, got):
    half = shape(PACKED // 2, RANK)
    return call(halves_kernel, (half, half), [VMEM, VMEM])(keep, got)


def sum_kernel(a_ref, b_ref, out_ref):
    out_ref[...] = a_ref[...] + b_ref[...]


def added(a, b):
    return call(sum_kernel, shape(*a.shape), [VMEM, VMEM])(a, b)


def inverse_factor(x):
    count = HALF // LANES
    tile = (LANES, HALF)
    rows = [x[LANES * q : LANES * (q + 1)] for q in range(count)]
    sub = lax.broadcasted_iota(jnp.int32, tile, 0)
    lane = lax.broadcasted_iota(jnp.int32, tile, 1)
    done = []
    for p in range(count):
        k = LANES * p
        cols = [
            [jnp.broadcast_to(rows[q][:, k + c : k + c + 1], tile) for q in range(p, count)]
            for c in range(LANES)
        ]
        panel = (lane >= k) & (lane < k + LANES)
        rows[p] = jnp.where(panel, jnp.where(lane - k == sub, 1.0, 0.0), rows[p])
        for q in range(p + 1, count):
            rows[q] = jnp.where(panel, 0.0, rows[q])
        scale = jnp.zeros(tile, F32)
        for i in range(LANES):
            pivot = jnp.broadcast_to(cols[i][0][i : i + 1], tile)
            inverse = 1.0 / pivot
            scale = jnp.where(sub == i, pivot, scale)
            factor = [v * inverse for v in cols[i]]
            factor[0] = jnp.where(sub > i, factor[0], 0.0)
            for c in range(i + 1, LANES):
                row = jnp.broadcast_to(cols[c][0][i : i + 1], tile)
                for q in range(count - p):
                    cols[c][q] = cols[c][q] - factor[q] * row
            row = jnp.broadcast_to(rows[p][i : i + 1], tile)
            for q in range(count - p):
                rows[p + q] = rows[p + q] - factor[q] * row
        done.append(jnp.where(lane < k + LANES, rows[p] * lax.rsqrt(scale), 0.0))
    return jnp.concatenate(done, 0)


def draw_kernel(counts, slots, mine_ref, other_ref, wu_ref, wi_ref, *refs):
    count = len(slots)
    fars, out_ref, nears, sems = refs[:count], refs[count], refs[count + 1 : -1], refs[-1]
    copies = fetches(slots, fars, nears, sems)
    for copy in copies:
        copy.start()
    first = parity() == 0
    lower = upper_half() == 0
    n = jnp.where(first, counts[0], counts[1])
    mine, other = mine_ref[...], other_ref[...]
    packed = jnp.concatenate(
        [jnp.where(lower, mine, other), jnp.where(lower, other, mine)], 0
    )
    bartlett_top = jnp.where(first, wu_ref[0:HALF], wi_ref[0:HALF])
    bartlett_low = jnp.where(first, wu_ref[HALF:], wi_ref[HALF:])
    mean = packed[HALF : HALF + 8] / n
    outer = dot(mean * 0.125, mean, 0, 0, HIGHEST)
    factor = n * n / (2.0 + n)
    upper, diagonal = corner()
    eye = jnp.where(diagonal, 1.0, 0.0)
    mixed = packed[0:HALF, 0:HALF]
    above = jnp.where(upper & ~diagonal, mixed, 0.0)
    below = jnp.where(upper, 0.0, mixed)
    line = jnp.broadcast_to(packed[HALF + 8 : HALF + 9, 0:HALF], (HALF, HALF))
    gram11 = jnp.where(upper, mixed, above.T)
    gram22 = jnp.where(diagonal, line, below + below.T)
    s11 = eye + gram11 - factor * outer[0:HALF, 0:HALF]
    s21 = packed[0:HALF, HALF:].T - factor * outer[HALF:, 0:HALF]
    s22 = eye + gram22 - factor * outer[HALF:, HALF:]
    g1 = inverse_factor(s11)
    l21 = dot(s21, g1, 1, 1, HIGHEST)
    s22 = s22 - dot(l21, l21, 1, 1, HIGHEST)
    top = dot(g1, bartlett_top, 0, 0, HIGHEST)
    carry = dot(l21, g1, 1, 0, HIGHEST)
    g2 = inverse_factor(s22)
    low = dot(g2, bartlett_low, 0, 0, HIGHEST)
    top = top - dot(carry, low, 0, 0, HIGHEST)
    both = jnp.concatenate([top, low], 0)
    out_ref[0:RANK] = dot(both, both, 1, 1, HIGHEST)
    out_ref[RANK:] = n * mean / (2.0 + n)
    for copy in copies:
        copy.wait()


def draw(counts, mine, other, wishart_user, wishart_item, later):
    slots, fars = zip(*later)
    drawn, *nears = call(
        functools.partial(draw_kernel, counts, slots),
        (shape(RANK + 8, RANK), *near_shapes(later)),
        [VMEM] * 4 + [ANY] * len(later),
        [fetch_sems(later)],
    )(mine, other, wishart_user, wishart_item, *fars)
    return drawn, nears


def prior_of(users, mine_ref, other_ref):
    take = parity() == (0 if users else 1)
    precision = jnp.where(take, mine_ref[0:RANK], other_ref[0:RANK])
    center = jnp.where(take, mine_ref[RANK : RANK + 1], other_ref[RANK : RANK + 1])
    return split_rows(precision), center


def residue_into(res_ref, at, ratings_ref, mask_ref, substep, row, rows, low_u, low_w):
    predicted = dot(low_u, low_w, 1, 1)
    for a in range(rows // TILE):
        for j in range(low_w.shape[0] // TILE):
            ra = slice(at + a * TILE, at + (a + 1) * TILE)
            pa = slice(a * TILE, (a + 1) * TILE)
            ij = slice(j * TILE, (j + 1) * TILE)
            t = (row + at) // TILE + a
            seen = mask_ref[substep, j : j + 1, t : t + 1].astype(F32)
            gap = ratings_ref[ra, ij].astype(F32) - predicted[pa, ij]
            res_ref[ra, ij] = (gap * seen).astype(BF16)


def first_kernel(weight, row, slots, noisy, mask_ref, ratings_ref, r_ref, u_ref, w_ref, *refs):
    un_ref, refs = (refs[0], refs[1:]) if noisy else (None, refs)
    count = len(slots)
    fars, (rt_ref, acc_ref) = refs[:count], refs[count : count + 2]
    nears = refs[count + 2 : 2 * count + 2]
    res_ref, low_ref, sems = refs[2 * count + 2 :]
    copies = fetches(slots, fars, nears, sems)
    for copy in copies:
        copy.start()
    low_w = w_ref[...].astype(BF16)
    total = rt_ref.shape[0]
    here = slice(row, row + total)
    low_ref[...] = u_ref[here].astype(BF16)
    rows = 256
    for t in range(total // rows):
        low_u = low_ref[t * rows : (t + 1) * rows]
        residue_into(
            res_ref, t * rows, ratings_ref.at[here], mask_ref, 0, row, rows, low_u, low_w
        )
    acc_ref[...] = dot(low_ref[...], res_ref[...], 0, 0)
    like_u = dot(res_ref[...], low_w, 1, 0)
    if un_ref is None:
        for copy in copies:
            copy.wait()
        un_ref = nears[0]
        copies = []
    rt_ref[...] = (
        DECAY * r_ref[here]
        + RATE * weight * like_u
        + jnp.sqrt(0.4) * un_ref[here].astype(F32)
    )
    for copy in copies:
        copy.wait()


def first_part(weight, row, rows, mask, ratings, user_mom, users, items, noise, later):
    k = users.shape[1]
    ni = items.shape[0]
    slots = tuple(slot for slot, _ in later)
    fars = [far for _, far in later]
    noise = [] if noise is None else [noise]
    rt, acc, *nears = call(
        functools.partial(first_kernel, weight, row, slots, len(noise)),
        (shape(rows, k), shape(k, ni), *near_shapes(later)),
        [VMEM] * 5 + [VMEM] * len(noise) + [ANY] * len(fars),
        [pltpu.VMEM((rows, ni), BF16), pltpu.VMEM((rows, k), BF16), fetch_sems(later)],
    )(mask, ratings, user_mom, users, items, *noise, *fars)
    return rt, acc, nears


def item_start_kernel(weight, w_ref, q_ref, in_ref, *refs):
    accs, out_ref = refs[:-1], refs[-1]
    like = accs[0][...]
    for acc in accs[1:]:
        like = like + acc[...]
    ni = w_ref.shape[0]
    out_ref[0:ni] = w_ref[...]
    out_ref[ni:] = (
        DECAY * q_ref[...] + RATE * weight * like.T + jnp.sqrt(0.4) * in_ref[...].astype(F32)
    )


def item_start(weight, items, item_mom, item_noise, accs):
    ni, k = item_mom.shape
    return call(
        functools.partial(item_start_kernel, weight),
        shape(2 * ni, k),
        [VMEM] * (3 + len(accs)),
    )(items, item_mom, item_noise, *accs)


def finish_kernel(mine_ref, other_ref, x_ref, *refs):
    parts, (x_out, m_out, item_ref, rhs_ref) = refs[:-4], refs[-4:]
    item_ref[...] = prior_of(False, mine_ref, other_ref)[0]
    rhs, center = prior_of(True, mine_ref, other_ref)
    rhs_ref[...] = rhs
    rows = 256
    base = 0
    for part in parts:
        for at in range(0, part.shape[0], rows):
            here = slice(base, base + rows)
            x = x_ref[here]
            columns = jnp.concatenate(split_columns(x - center), 1)
            m = part[at : at + rows] + RATE * dot(columns, rhs_ref[...], 1, 0)
            m_out[here] = m
            x_out[here] = x + RATE * m
            base += rows


def finish(mine, other, x, parts):
    n, k = x.shape
    return call(
        finish_kernel,
        (shape(n, k), shape(n, k), shape(6 * RANK, k, BF16)),
        [VMEM] * (3 + len(parts)),
        [pltpu.VMEM((6 * RANK, k), BF16)],
    )(mine, other, x, *parts)


def first_items_kernel(mine_ref, other_ref, rhs_ref, pack_ref, w_out, q_out):
    row = slice(RANK, RANK + 1)
    center = jnp.where(parity() == 1, mine_ref[row], other_ref[row])
    ni = w_out.shape[0]
    w = pack_ref[0:ni]
    prior = dot(jnp.concatenate(split_columns(w - center), 1), rhs_ref[...], 1, 0)
    q = pack_ref[ni:] + RATE * prior
    q_out[...] = q
    w_out[...] = w + RATE * q


def first_items(mine, other, rhs, pack):
    ni, k = pack.shape[0] // 2, pack.shape[1]
    return call(first_items_kernel, (shape(ni, k),) * 2, [VMEM] * 4)(mine, other, rhs, pack)


def items_kernel(weight, substep, turn, mask_ref, mine_ref, other_ref, *refs):
    ratings_ref, u_ref, in_ref, w_ref, q_ref = refs[:5]
    res_ref, out_ref, low_ref, part_ref = refs[-4:]

    def work():
        rhs, center = prior_of(False, mine_ref, other_ref)
        ni = in_ref.shape[0]
        w, q = w_ref[...], q_ref[...]
        if turn is not None:
            w = w + RATE * q
            out_ref[0:ni] = w
        prior = dot(jnp.concatenate(split_columns(w - center), 1), rhs, 1, 0)
        part_ref[...] = DECAY * q + RATE * prior + jnp.sqrt(0.4) * in_ref[...].astype(F32)
        low_w = w.astype(BF16)
        rows = 256
        for t in range(u_ref.shape[0] // rows):
            here = slice(t * rows, (t + 1) * rows)
            low_u = u_ref[here].astype(BF16)
            low_ref[here] = low_u
            residue_into(
                res_ref, t * rows, ratings_ref, mask_ref, substep, 0, rows, low_u, low_w
            )
        like = dot(low_ref[...], res_ref[...], 0, 0)
        out_ref[out_ref.shape[0] - ni :] = part_ref[...] + RATE * weight * like.T

    if turn is None:
        work()
    else:
        pl.when(parity() == turn)(work)


def items_step(weight, substep, turn, mask, mine, other, ratings, users, noise, w, q, res=None):
    n, k = users.shape
    ni = noise.shape[0]
    more = [] if res is None else [res]
    return call(
        functools.partial(items_kernel, weight, substep, turn),
        (shape(n, ni, BF16), shape(ni if turn is None else 2 * ni, k)),
        [VMEM] * (8 + len(more)),
        [pltpu.VMEM((n, k), BF16), pltpu.VMEM((ni, k), F32)],
        aliases={8: 0} if more else {},
    )(mask, mine, other, ratings, users, noise, w, q, *more)


def users_kernel(
    weight,
    slots,
    mine_ref,
    other_ref,
    res_ref,
    u_ref,
    r_ref,
    un_ref,
    even_ref,
    odd_ref,
    *refs,
):
    if slots:
        count = len(slots)
        fars, (u_out, r_out), nears = refs[:count], refs[count : count + 2], refs[count + 2 : -2]
        rhs_ref, sems = refs[-2:]
        copies = fetches(slots, fars, nears, sems)
    else:
        (u_out, r_out, *draws), rhs_ref, copies = refs[:-1], refs[-1], []
    for copy in copies:
        copy.start()
    if not slots:
        mine, other = mine_ref[0:RANK], other_ref[0:RANK]
        first = parity() == 0
        draws[0][...] = jnp.where(first, mine, other)
        draws[1][...] = jnp.where(first, other, mine)
    ni = res_ref.shape[1]
    rhs_ref[0:ni] = jnp.where(parity() == 0, even_ref[0:ni], odd_ref[0:ni]).astype(BF16)
    rhs, center = prior_of(True, mine_ref, other_ref)
    rhs_ref[ni:] = rhs
    rows = 256
    for t in range(u_ref.shape[0] // rows):
        here = slice(t * rows, (t + 1) * rows)
        x = u_ref[here]
        columns = jnp.concatenate(split_columns(x - center), 1)
        like = dot(res_ref[here], rhs_ref[0:ni], 1, 0)
        r = (
            DECAY * r_ref[here]
            + RATE * (weight * like + dot(columns, rhs_ref[ni:], 1, 0))
            + jnp.sqrt(0.4) * un_ref[here].astype(F32)
        )
        r_out[here] = r
        u_out[here] = x + RATE * r
    for copy in copies:
        copy.wait()


def users_step(weight, later, mine, other, res, even, odd, users, user_mom, user_noise):
    n, k = users.shape
    ni = res.shape[1]
    slots = tuple(slot for slot, _ in later)
    fars = [far for _, far in later]
    more = near_shapes(later) if later else [shape(RANK, RANK)] * 2
    return call(
        functools.partial(users_kernel, weight, slots),
        (shape(n, k), shape(n, k), *more),
        [VMEM] * 8 + [ANY] * len(fars),
        [pltpu.VMEM((ni + 6 * RANK, k), BF16)] + [fetch_sems(later)] * bool(later),
        near=bool(later),
    )(mine, other, res, users, user_mom, user_noise, even, odd, *fars)


def arrived_kernel(even_ref, odd_ref, w_out, q_out, w_ref, sems):
    ni = w_ref.shape[0]

    def run(pack_ref):
        first = pltpu.make_async_copy(pack_ref.at[pl.ds(ni, ni)], q_out, sems.at[0])
        first.start()
        w_ref[...] = pack_ref[0:ni] + RATE * pack_ref[ni:]
        second = pltpu.make_async_copy(w_ref, w_out, sems.at[1])
        second.start()
        first.wait()
        second.wait()

    pl.when(parity() == 0)(lambda: run(even_ref))
    pl.when(parity() == 1)(lambda: run(odd_ref))


def arrived(even, odd):
    ni, k = even.shape[0] // 2, even.shape[1]
    out = pltpu.HBM((ni, k), F32)
    near = lambda x: pltpu.with_memory_space_constraint(x, pltpu.VMEM)
    return pl.pallas_call(
        arrived_kernel,
        out_shape=(out, out),
        in_specs=[VMEM, VMEM],
        out_specs=(ANY, ANY),
        scratch_shapes=[pltpu.VMEM((ni, k), F32), pltpu.SemaphoreType.DMA((2,))],
        compiler_params=params(),
        cost_estimate=pl.CostEstimate(flops=1000, bytes_accessed=1000, transcendentals=0),
    )(near(even), near(odd))


def swapped(array, by, size):
    return lax.ppermute(array, "blk", [(i, i ^ by) for i in range(size)])


def local(
    ratings,
    tile_mask,
    user_factors,
    user_momentum,
    item_factors,
    item_momentum,
    user_noise,
    item_noise,
    wishart_user,
    wishart_item,
):
    blocks = lax.axis_size("blk")
    user_rows = user_factors.shape[0]
    item_rows = item_factors.shape[0]
    weight = 1.0 * blocks
    fence = lax.optimization_barrier
    inside = [(i, i ^ 1) for i in range(blocks)]
    across = [(i, (i - 1) % blocks) for i in range(0, blocks, 2)]
    ring = [(i, (i - 1) % blocks) for i in range(blocks)]

    mask = tile_mask.transpose(0, 2, 1)
    parts = 4
    rows = user_rows // parts
    rts, accs, loaded = [], [], []
    later = [
        [(0, user_noise)],
        [(None, item_momentum), (0, item_noise)],
        [(None, wishart_user), (None, wishart_item)],
        [],
    ]

    keep, send, near_u, near_w, near_ratings, near_r, mask = grams(
        user_factors,
        item_factors,
        [(0, ratings), (None, user_momentum), (None, mask)],
    )
    got = swapped(send, 1, blocks)
    mine, send = halves(keep, got)

    def part():
        j = len(rts)
        rt, acc, nears = first_part(
            weight,
            j * rows,
            rows,
            mask,
            near_ratings,
            near_r,
            near_u,
            near_w,
            loaded[0][0] if j else None,
            later[j],
        )
        rts.append(rt)
        accs.append(acc)
        loaded.append(nears)

    by = 2
    while by < blocks:
        send, near_u = fence((send, near_u))
        got = swapped(send, by, blocks)
        if len(rts) < parts:
            part()
            got, rts[-1], accs[-1] = fence((got, rts[-1], accs[-1]))
        mine = added(mine, got)
        send = mine
        by = by * 2
    send, near_u = fence((send, near_u))
    other = swapped(send, 2, blocks)
    while len(rts) < parts:
        part()
    item_part = item_start(weight, near_w, *loaded[1], accs)
    other, item_part, *rts = fence((other, item_part, *rts))
    send = lambda array, pairs: lax.ppermute(array, "blk", pairs)
    early = send(item_part, ring)
    wu, wi = loaded[2]
    counts = (1.0 * user_rows * blocks, 1.0 * item_rows * blocks)
    later = [(1, x) for x in (ratings, user_noise, item_noise)]
    drawn, near = draw(counts, mine, other, wu, wi, later)
    peer = swapped(drawn, 1, blocks)
    users, user_mom, split_item = finish(drawn, peer, near_u, rts)
    users, early = fence((users, early))
    items, item_mom = first_items(drawn, peer, split_item, early)

    before = send(items, ring)
    args = (mask, drawn, peer, near[0], users, near[2])
    res, item_mom = items_step(weight, 1, None, *args, items, item_mom)
    q_even, q_odd = send(item_mom, inside), send(item_mom, across)
    later = [(2, x) for x in (ratings, user_noise, item_noise)]
    users, user_mom, *near = users_step(
        weight, later, drawn, peer, res, items, items, users, user_mom, near[1]
    )
    before, users, user_mom, *near = fence((before, users, user_mom, *near))

    args = (mask, drawn, peer, near[0], users, near[2])
    res, even = items_step(weight, 2, 0, *args, before, q_even)
    pack_odd = send(even, across)
    res, odd = items_step(weight, 2, 1, *args, before, q_odd, res)
    pack_even = send(odd, inside)
    users, user_mom, *precisions = users_step(
        weight, [], drawn, peer, res, even, odd, users, user_mom, near[1]
    )
    pack_odd, users, user_mom, *precisions = fence((pack_odd, users, user_mom, *precisions))
    items, item_mom = arrived(pack_even, pack_odd)
    return (users, user_mom, items, item_mom, *precisions)


def solution(mesh):
    placed = (
        P(None, ("chain", "blk"), None),
        P(None, ("chain", "blk"), None),
        P(("chain", "blk"), None),
        P(("chain", "blk"), None),
        P(("chain", "blk"), None),
        P(("chain", "blk"), None),
        P(None, ("chain", "blk"), None),
        P(None, ("chain", "blk"), None),
        P("chain", None),
        P("chain", None),
    )
    return jax.shard_map(
        local,
        mesh=mesh,
        in_specs=placed,
        out_specs=(
            P(("chain", "blk"), None),
            P(("chain", "blk"), None),
            P(("chain", "blk"), None),
            P(("chain", "blk"), None),
            P("chain", None),
            P("chain", None),
        ),
        check_vma=False,
    )
```
